32 devices in a mesh: rep: 4 (over z), fsdp: 8 (over y, x, core).
Axes of the slice: x: 2, y: 2, z: 4, core: 2. Of those that a mesh axis runs over, the one named last changes fastest.
Arguments:
- inputs: bfloat16 [32, 1024, 1024], P(('rep', 'fsdp')), may hold values from -6 to 6
- lengths: int32 [32], P(('rep', 'fsdp')), may hold values from 800 to 1024
- bucket_table: int32 [1024], replicated, may hold values from 0 to 31, as said below
- ln1_gain: bfloat16 [1024], P('fsdp'), may hold values from 0.099609375 to 1.8984375
- ln1_shift: bfloat16 [1024], P('fsdp'), may hold values from -3 to 3
- w_qkv: bfloat16 [1024, 3072], P('fsdp'), may hold values from -0.1875 to 0.1875
- rel_bias: bfloat16 [512], P('fsdp'), may hold values from -4 to 4
- w_out: bfloat16 [1024, 1024], P('fsdp'), may hold values from -3 to 3
- ln2_gain: bfloat16 [1024], P('fsdp'), may hold values from 0.099609375 to 1.8984375
- ln2_shift: bfloat16 [1024], P('fsdp'), may hold values from -3 to 3
- w_in: bfloat16 [1024, 4096], P('fsdp'), may hold values from -0.1875 to 0.1875
- w_down: bfloat16 [4096, 1024], P('fsdp'), may hold values from -0.09375 to 0.09375
- cotangent: bfloat16 [32, 1024, 1024], P(('rep', 'fsdp')), may hold values from -6 to 6
Outputs:
- outputs: bfloat16 [32, 1024, 1024], P(('rep', 'fsdp'))
- input_grad: float32 [32, 1024, 1024], P(('rep', 'fsdp'))
- ln1_gain_grad: float32 [1024], P('fsdp')
- ln1_shift_grad: float32 [1024], P('fsdp')
- w_qkv_grad: float32 [1024, 3072], P('fsdp')
- rel_bias_grad: float32 [512], P('fsdp')
- w_out_grad: float32 [1024, 1024], P('fsdp')
- ln2_gain_grad: float32 [1024], P('fsdp')
- ln2_shift_grad: float32 [1024], P('fsdp')
- w_in_grad: float32 [1024, 4096], P('fsdp')
- w_down_grad: float32 [4096, 1024], P('fsdp')
The draws below stay inside these ranges and needn't reach their ends.
Inputs may be any that keep to these rules, and one draw needn't show every extreme that they name: bucket_table[k] = k for k < 16; it never falls as k grows and takes every value from 0 to 31.
All inputs are finite; a program needn't handle non-finite values.
Results may differ from the reference program's by a relative error of at most 0.017.
Values may be sent and summed in bfloat16 or wider, within the bound.
No kernel may reach another device: no remote copies, remote signals or barrier semaphores. Data moves between devices by JAX's collectives and lax.ppermute only.
A program may use at most 512 MiB of HBM per device.

```python
import jax
import jax.numpy as jnp
from jax import lax

D = 1024
HEADS = 16
HEAD_DIM = 64
FF = 4096
BUCKETS = 32
SLOTS = 1024
CLIPS = 32


def draw_bucket_table(key, part):
    half_count = BUCKETS // 2
    span_count = SLOTS - half_count - 1
    shuffled = jax.random.permutation(key, span_count)
    breaks = jnp.sort(shuffled[:half_count - 1]) + half_count + 1
    distance = jnp.arange(SLOTS, dtype=jnp.int32)
    far_bucket = half_count + jnp.sum((distance[:, None] >= breaks[None, :]).astype(jnp.int32), axis=1)
    return jnp.where(distance < half_count, distance, far_bucket).astype(jnp.int32)


def place_ends(values, key, least, high):
    index_at = [jax.random.randint(jax.random.fold_in(key, axis), (), 0, length) for axis, length in enumerate(values.shape)]
    main_axis = values.shape.index(max(values.shape))
    next_to = index_at[:main_axis] + [(index_at[main_axis] + 1) % values.shape[main_axis]] + index_at[main_axis + 1:]
    return values.at[tuple(index_at)].set(least).at[tuple(next_to)].set(high)


def strengthened(entries, key, source, target, blocks, factor):
    owner, partner = [(jnp.arange(entries.shape[dim]) // (entries.shape[dim] // blocks)).reshape([-1 if axis == dim else 1 for axis in range(entries.ndim)]) for dim in (source, target)]
    chosen = jax.random.permutation(key, blocks)[partner]
    strong = (owner == chosen) | (owner == (partner + blocks // 2) % blocks)
    return jnp.where(strong, factor * entries, entries)


def level_of(key, dims, shards, smallest, high):
    level, own = 1.0, jax.random.fold_in(key, 6)
    for dim, blocks in shards:
        steps = jnp.exp(jax.random.uniform(jax.random.fold_in(own, dim), (blocks,), jnp.float32, smallest / len(shards), high / len(shards)))
        level = level * jnp.repeat(steps, dims[dim] // blocks).reshape([-1 if axis == dim else 1 for axis in range(len(dims))])
    return level


def noise(rng, extent, width, reach, split=(), kind=jnp.bfloat16):
    loudness = level_of(rng, extent, split, -0.22, 0.18) if split else 1.0
    drawn = jax.random.normal(rng, extent, jnp.float32) * width * loudness
    return jnp.minimum(jnp.maximum(drawn, -reach), reach).astype(kind)


def heavy_noise(key, extent, scale, reach, split, heavy, kind=jnp.bfloat16):
    drawn = scale * jax.random.normal(key, extent, jnp.float32)
    if split:
        drawn = drawn * level_of(key, extent, split, -0.22, 0.18)
    return jnp.clip(strengthened(drawn, jax.random.fold_in(key, 3), *heavy), -reach, reach).astype(kind)


def setup_inputs(seed: int = 0) -> dict:
    keys = jax.random.split(jax.random.key(seed), 14)
    inputs = heavy_noise(keys[0], (CLIPS, SLOTS, D), 1.0, 6.0, ((0, 32),), (0, 2, 32, 2.75))
    lengths = place_ends(jax.random.randint(keys[1], (CLIPS,), SLOTS * 25 // 32, SLOTS + 1), jax.random.fold_in(keys[1], 1), SLOTS * 25 // 32, SLOTS).astype(jnp.int32)
    bucket_table = draw_bucket_table(jax.random.fold_in(keys[13], 71), 0)
    ln1_gain = jnp.clip(1.0 + 0.18 * jax.random.normal(keys[3], (D,), jnp.float32), 0.099609375, 1.8984375).astype(jnp.bfloat16)
    ln1_shift = noise(keys[4], (D,), 0.5, 3.0, ((0, 8),))
    w_qkv = noise(keys[5], (D, 3 * D), D ** -0.5, 0.1875, ((0, 8),))
    rel_bias = noise(keys[6], (HEADS * BUCKETS,), 1.0, 4.0, ((0, 8),))
    w_out = noise(keys[7], (D, D), (max(D // 256, 1)) ** -0.5, 3.0, ((0, 8),))
    ln2_gain = jnp.clip(1.0 + 0.18 * jax.random.normal(keys[8], (D,), jnp.float32), 0.099609375, 1.8984375).astype(jnp.bfloat16)
    ln2_shift = noise(keys[9], (D,), 0.5, 3.0, ((0, 8),))
    w_in = noise(keys[10], (D, FF), D ** -0.5, 0.1875, ((0, 8),))
    w_down = noise(keys[11], (FF, D), FF ** -0.5, 0.09375, ((0, 8),))
    cotangent = noise(keys[12], (CLIPS, SLOTS, D), 1.0, 6.0, ((0, 32),))
    return {"inputs": inputs, "lengths": lengths, "bucket_table": bucket_table, "ln1_gain": ln1_gain, "ln1_shift": ln1_shift, "w_qkv": w_qkv, "rel_bias": rel_bias, "w_out": w_out, "ln2_gain": ln2_gain, "ln2_shift": ln2_shift, "w_in": w_in, "w_down": w_down, "cotangent": cotangent}


@jax.custom_vjp
def low(v):
    return lax.optimization_barrier(v.astype(jnp.bfloat16)).astype(jnp.float32)

@jax.custom_vjp
def low_back(v):
    return v

def low_keep(v):
    return (low(v), None)

def low_pass(kept, grad):
    return (grad,)

def back_keep(v):
    return (v, None)

def back_low(kept, grad):
    return (low(grad),)
low.defvjp(low_keep, low_pass)
low_back.defvjp(back_keep, back_low)

def both_ways(values):
    return low(low_back(values))

def matmul(left, right):
    return jnp.dot(left, right, precision=lax.Precision.HIGHEST, preferred_element_type=jnp.float32)

def layer_norm(values, gain_row, shift_row):
    average = lax.optimization_barrier(jnp.mean(values, axis=-1, keepdims=True))
    centred = values - average
    spread = lax.optimization_barrier(jnp.mean(centred * centred, axis=-1, keepdims=True))
    return centred * lax.rsqrt(spread + 1e-05) * gain_row + shift_row

def gelu_exact(values):
    return jax.nn.gelu(values, approximate=False)

def clip_forward(residual, clip_length, bucket_table, params):
    gain_one, shift_one, qkv_weight, table_flat, out_weight, gain_two, shift_two, in_weight, down_weight = params
    slot_count = residual.shape[0]
    score_scale = HEAD_DIM ** (-0.5)
    normed_one = low(layer_norm(residual, gain_one, shift_one))
    projected = both_ways(matmul(normed_one, qkv_weight))
    queries = projected[:, :D].reshape(slot_count, HEADS, HEAD_DIM)
    key_rows = projected[:, D:2 * D].reshape(slot_count, HEADS, HEAD_DIM)
    value_rows = projected[:, 2 * D:].reshape(slot_count, HEADS, HEAD_DIM)
    raw_scores = jnp.einsum('ihd,jhd->hij', queries, key_rows, precision=lax.Precision.HIGHEST)
    slot_ids = lax.iota(jnp.int32, slot_count)
    distance = jnp.maximum(slot_ids[:, None] - slot_ids[None, :], 0)
    table_heads = table_flat.reshape(HEADS, BUCKETS)
    bias_full = table_heads[:, bucket_table[distance]]
    scores = low_back(raw_scores * score_scale + bias_full)
    allowed = (slot_ids[None, :] <= slot_ids[:, None]) & (slot_ids[None, :] < clip_length)
    probs = low(jax.nn.softmax(jnp.where(allowed[None], scores, -1e+30), axis=-1))
    attended = jnp.einsum('hij,jhd->ihd', probs, value_rows, precision=lax.Precision.HIGHEST)
    attended = both_ways(attended.reshape(slot_count, D))
    middle = residual + low_back(matmul(attended, out_weight))
    normed_two = low(layer_norm(middle, gain_two, shift_two))
    hidden_pre = low_back(matmul(normed_two, in_weight))
    hidden = low(gelu_exact(hidden_pre))
    ffn_out = low_back(matmul(hidden, down_weight))
    valid = (slot_ids < clip_length).astype(jnp.float32)[:, None]
    return (middle + ffn_out) * valid

def reference(inputs, lengths, bucket_table, ln1_gain, ln1_shift, w_qkv, rel_bias, w_out, ln2_gain, ln2_shift, w_in, w_down, cotangent):
    params = tuple((item.astype(jnp.float32) for item in (ln1_gain, ln1_shift, w_qkv, rel_bias, w_out, ln2_gain, ln2_shift, w_in, w_down)))
    residual = inputs.astype(jnp.float32)
    group_size = 4

    def forward(residual, params):
        grouped = residual.reshape(CLIPS // group_size, group_size, SLOTS, D)
        grouped_len = lengths.reshape(CLIPS // group_size, group_size)

        def group_step(carry, item):
            block_rows, block_len = item
            result = jax.vmap(lambda clip_rows, clip_len: clip_forward(clip_rows, clip_len, bucket_table, params))(block_rows, block_len)
            return (carry, result)
        unused, result = lax.scan(jax.checkpoint(group_step), jnp.zeros((), jnp.float32), (grouped, grouped_len))
        return result.reshape(CLIPS, SLOTS, D)
    outputs, pullback = jax.vjp(forward, residual, params)
    input_grad, grads = pullback(cotangent.astype(jnp.float32))
    return (outputs.astype(jnp.bfloat16), input_grad, grads[0], grads[1], grads[2], grads[3], grads[4], grads[5], grads[6], grads[7], grads[8])
```

```python
import jax
import jax.numpy as jnp
from jax import lax
from jax.experimental import pallas as pl
from jax.experimental.pallas import tpu as pltpu
from jax.sharding import PartitionSpec as P

HEADS = 16
HEAD_DIM = 64
BUCKETS = 32
T = 256
NEG = -1e30
F32 = jnp.float32
BF = jnp.bfloat16

def layer_norm(values, gain_row, shift_row):
    average = jnp.mean(values, axis=-1, keepdims=True)
    centred = values - average
    spread = jnp.mean(centred * centred, axis=-1, keepdims=True)
    return centred * lax.rsqrt(spread + 1e-05) * gain_row + shift_row


def gelu_exact(values):
    return jax.nn.gelu(values, approximate=False)


def bucket_onehot(bucket_table, bucket_count):
    return (bucket_table[:, None] == lax.iota(jnp.int32, bucket_count)[None, :]).astype(
        jnp.bfloat16
    )


def toeplitz(base_ref):
    row=lax.broadcasted_iota(jnp.int32,(T,T),0); col=lax.broadcasted_iota(jnp.int32,(T,T),1)
    upper = col>=row
    rolled=[]
    for U in range(4):
        a=jnp.broadcast_to(base_ref[0,U:U+1,:],(T,T))
        rolled.append(pltpu.roll(a,0,1,stride=1,stride_axis=0))
    out=[]
    for U in range(4):
        nxt = rolled[U+1] if U<3 else NEG
        out.append(jnp.where(upper,rolled[U],nxt))
    return out

def fwd_kernel(len_ref, base_ref, qT_ref, kT_ref, vT_ref, oT_ref, lt_ref, g_ref):
    for U,t in enumerate(toeplitz(base_ref)): g_ref[U*T:(U+1)*T,:]=t
    k = kT_ref[0].T
    vT= vT_ref[0]
    kid = 768+lax.broadcasted_iota(jnp.int32,(T,1),0)
    kmask = jnp.where(kid<len_ref[0],0.0,NEG).astype(F32)
    for bi in range(4):
        nk=(bi+1)*T
        qT=qT_ref[0,:,bi*T:(bi+1)*T]*BF(0.125)
        s=jnp.dot(k[:nk],qT,preferred_element_type=F32)+g_ref[(3-bi)*T:,:]
        if bi==3:
            s=jnp.concatenate([s[:768],s[768:]+kmask],axis=0)
        m=jnp.max(s,axis=0,keepdims=True)
        p=jnp.exp(s-m)
        l=jnp.sum(p,axis=0,keepdims=True)
        o=jnp.dot(vT[:,:nk],p.astype(BF),preferred_element_type=F32)
        oT_ref[0,:,bi*T:(bi+1)*T]=(o*(1.0/l)).astype(BF)
        lt_ref[0,:,bi*T:(bi+1)*T]=m+jnp.log(l)

def attn_fwd(length, base, qkvT, vmem=48<<20):
    hs=lambda off: pl.BlockSpec((1,64,1024),lambda h:(h+off,0,0))
    return pl.pallas_call(fwd_kernel, grid=(16,),
        in_specs=[pl.BlockSpec(memory_space=pltpu.SMEM), pl.BlockSpec((1,4,T),lambda h:(h,0,0)), hs(0),hs(16),hs(32)],
        out_specs=[pl.BlockSpec((1,64,1024),lambda h:(h,0,0)), pl.BlockSpec((1,1,1024),lambda h:(h,0,0))],
        out_shape=[jax.ShapeDtypeStruct((16,64,1024),BF),jax.ShapeDtypeStruct((16,1,1024),F32)],
        scratch_shapes=[pltpu.VMEM((1024,T),F32)],
        compiler_params=pltpu.CompilerParams(vmem_limit_bytes=vmem),
    )(length, base, qkvT,qkvT,qkvT)

def bwd_kernel(len_ref, base_ref, qT_ref, kT_ref, vT_ref, oT_ref, doT_ref, lt_ref, dq_ref, dk_ref, dv_ref, dist_ref, g_ref, dg_ref, dkv, dvv):
    for U,t in enumerate(toeplitz(base_ref)): g_ref[U*T:(U+1)*T,:]=t
    kT=kT_ref[0]
    k=kT.T; v=vT_ref[0].T
    kid = 768+lax.broadcasted_iota(jnp.int32,(T,1),0)
    kmask = jnp.where(kid<len_ref[0],0.0,NEG).astype(F32)
    for bi in (3,2,1,0):
        nk=(bi+1)*T
        sl=slice(bi*T,(bi+1)*T)
        qT=qT_ref[0,:,sl]*BF(0.125)
        doT=doT_ref[0,:,sl]
        inner=jnp.sum(doT.astype(F32)*oT_ref[0,:,sl].astype(F32),axis=0,keepdims=True)
        lt=lt_ref[0,:,sl]
        s=jnp.dot(k[:nk],qT,preferred_element_type=F32)+g_ref[(3-bi)*T:,:]
        if bi==3:
            s=jnp.concatenate([s[:768],s[768:]+kmask],axis=0)
        p=jnp.exp(s-lt)
        dp=jnp.dot(v[:nk],doT,preferred_element_type=F32)
        ds=p*(dp-inner)
        pb=p.astype(BF); dsb=ds.astype(BF)
        dq_ref[0,:,sl]=(jnp.dot(kT[:,:nk],dsb,preferred_element_type=F32)*0.125).astype(BF)
        dvp=lax.dot_general(doT,pb,(((1,),(1,)),((),())),preferred_element_type=F32)
        dkp=lax.dot_general(qT,dsb,(((1,),(1,)),((),())),preferred_element_type=F32)
        if bi==3:
            dkv[...]=dkp; dvv[...]=dvp; dg_ref[...]=ds
        else:
            dkv[:,:nk]+=dkp; dvv[:,:nk]+=dvp; dg_ref[(3-bi)*T:,:]+=ds
    dk_ref[0]=dkv[...].astype(BF); dv_ref[0]=dvv[...].astype(BF)
    skew_sums(dg_ref, dist_ref)

def skew_sums(dg_ref, dist_ref):
    row=lax.broadcasted_iota(jnp.int32,(T,T),0); col=lax.broadcasted_iota(jnp.int32,(T,T),1)
    upper = col>=row
    for V in range(4):
        cur=dg_ref[V*T:(V+1)*T,:]
        prev=dg_ref[(V-1)*T:V*T,:] if V else 0.0
        z=jnp.where(upper,cur,prev)
        acc=z[0:8]
        for g in range(1,T//8):
            acc=acc+pltpu.roll(z[8*g:8*g+8],T-8*g,1)
        tot=acc[0:1]
        for r in range(1,8):
            tot=tot+pltpu.roll(acc[r:r+1],T-r,1)
        dist_ref[0,V:V+1,:]=tot

def attn_bwd(length, base, qkvT, oT, doT, lt, vmem=48<<20):
    hs=lambda off: pl.BlockSpec((1,64,1024),lambda h:(h+off,0,0))
    return pl.pallas_call(bwd_kernel, grid=(16,),
        in_specs=[pl.BlockSpec(memory_space=pltpu.SMEM), pl.BlockSpec((1,4,T),lambda h:(h,0,0)), hs(0),hs(16),hs(32),hs(0),hs(0),pl.BlockSpec((1,1,1024),lambda h:(h,0,0))],
        out_specs=[hs(0),hs(0),hs(0), pl.BlockSpec((1,4,T),lambda h:(h,0,0))],
        out_shape=[jax.ShapeDtypeStruct((16,64,1024),BF)]*3+[jax.ShapeDtypeStruct((16,4,T),F32)],
        scratch_shapes=[pltpu.VMEM((1024,T),F32),pltpu.VMEM((1024,T),F32),pltpu.VMEM((64,1024),F32),pltpu.VMEM((64,1024),F32)],
        compiler_params=pltpu.CompilerParams(vmem_limit_bytes=vmem),
    )(length, base, qkvT,qkvT,qkvT,oT,doT,lt)


def per_device(inputs, lengths, bucket_table, ln1_gain, ln1_shift, w_qkv, rel_bias, w_out, ln2_gain, ln2_shift, w_in, w_down, cotangent):
    gather = lambda w: lax.all_gather(w, "fsdp", axis=0, tiled=True)
    small = gather(jnp.concatenate([ln1_gain, ln1_shift, ln2_gain, ln2_shift, rel_bias])[None])
    qkv_full = gather(w_qkv)
    out_full = gather(w_out)
    in_full = gather(w_in)
    down_full = gather(w_down)
    width = inputs.shape[-1]
    n = ln1_gain.shape[0]
    gain_one, shift_one, gain_two, shift_two = (small[:, i * n:(i + 1) * n].reshape(-1).astype(F32) for i in range(4))
    table_heads = small[:, 4 * n:].reshape(HEADS, BUCKETS)
    slots = inputs.shape[1]
    onehot = bucket_onehot(bucket_table, BUCKETS)
    by_distance = jnp.einsum("hb,sb->hs", table_heads, onehot, preferred_element_type=F32)
    base = by_distance.reshape(HEADS, slots // T, T)[:, ::-1]
    residual = inputs.reshape(slots, width).astype(F32)
    normed_one = layer_norm(residual, gain_one, shift_one).astype(BF)
    projT = jnp.einsum("rd,dc->cr", normed_one, qkv_full, preferred_element_type=F32).astype(BF)
    qkvT = projT.reshape(3 * HEADS, HEAD_DIM, slots)
    oT, log_total = attn_fwd(lengths, base, qkvT)
    attT = oT.reshape(width, slots)
    middle = residual + jnp.einsum("kr,kd->rd", attT, out_full, preferred_element_type=F32)
    normed_two = layer_norm(middle, gain_two, shift_two).astype(BF)
    hidden_pre = jnp.dot(normed_two, in_full, preferred_element_type=F32)
    hidden = gelu_exact(hidden_pre).astype(BF)
    ffn_out = jnp.dot(hidden, down_full, preferred_element_type=F32)
    valid = (lax.iota(jnp.int32, slots) < lengths[0]).astype(F32)[:, None]
    outputs = ((middle + ffn_out) * valid).astype(BF).reshape(inputs.shape)
    out_grad = cotangent.reshape(slots, width).astype(F32) * valid
    out_low = out_grad.astype(BF)
    down_grad = jnp.einsum("rf,rd->fd", hidden, out_low, preferred_element_type=F32)
    hidden_grad = jnp.einsum("rd,fd->rf", out_low, down_full, preferred_element_type=F32)
    pre_grad = jax.vjp(gelu_exact, hidden_pre)[1](hidden_grad)[0].astype(BF)
    in_grad = jnp.einsum("rd,rf->df", normed_two, pre_grad, preferred_element_type=F32)
    normed_two_grad = jnp.einsum("rf,df->rd", pre_grad, in_full, preferred_element_type=F32)
    middle_part, gain_two_grad, shift_two_grad = jax.vjp(layer_norm, middle, gain_two, shift_two)[1](normed_two_grad)
    middle_grad = out_grad + middle_part
    branch_grad = middle_grad.astype(BF)
    out_w_grad = jnp.einsum("kr,rd->kd", attT, branch_grad, preferred_element_type=F32)
    doT = jnp.einsum("kd,rd->kr", out_full, branch_grad, preferred_element_type=F32).astype(BF)
    dq, dk, dv, dist = attn_bwd(lengths, base, qkvT, oT, doT.reshape(HEADS, HEAD_DIM, slots), log_total)
    distance_total = dist[:, ::-1].reshape(HEADS, slots)
    table_grad = jnp.dot(distance_total, onehot.astype(F32), precision=lax.Precision.HIGHEST, preferred_element_type=F32)
    pgT = jnp.concatenate([dq, dk, dv], axis=0).reshape(3 * width, slots)
    qkv_grad = jnp.einsum("rd,er->de", normed_one, pgT, preferred_element_type=F32)
    normed_one_grad = jnp.einsum("er,de->rd", pgT, qkv_full, preferred_element_type=F32)
    input_part, gain_one_grad, shift_one_grad = jax.vjp(layer_norm, residual, gain_one, shift_one)[1](normed_one_grad)
    input_grad = (middle_grad + input_part).reshape(inputs.shape)
    def reduced(g):
        part = lax.psum_scatter(g.astype(BF), "fsdp", scatter_dimension=0, tiled=True)
        return lax.psum(part, "rep").astype(F32)
    groups = small.shape[0]
    packed = jnp.concatenate([v.reshape(groups, -1) for v in (gain_one_grad, shift_one_grad, gain_two_grad, shift_two_grad, table_grad)], axis=1)
    tiny = lax.psum(lax.psum_scatter(packed, "fsdp", scatter_dimension=0, tiled=True), "rep")[0]
    return (outputs, input_grad, tiny[:n], tiny[n:2 * n], reduced(qkv_grad), tiny[4 * n:], reduced(out_w_grad), tiny[2 * n:3 * n], tiny[3 * n:4 * n], reduced(in_grad), reduced(down_grad))


def solution(mesh):
    placed = (
        P(("rep", "fsdp"), None, None),
        P(("rep", "fsdp")),
        P(),
        P("fsdp"),
        P("fsdp"),
        P("fsdp", None),
        P("fsdp"),
        P("fsdp", None),
        P("fsdp"),
        P("fsdp"),
        P("fsdp", None),
        P("fsdp", None),
        P(("rep", "fsdp"), None, None),
    )
    return jax.shard_map(
        per_device,
        mesh=mesh,
        in_specs=placed,
        out_specs=(
            P(("rep", "fsdp"), None, None),
            P(("rep", "fsdp"), None, None),
            P("fsdp"),
            P("fsdp"),
            P("fsdp", None),
            P("fsdp"),
            P("fsdp", None),
            P("fsdp"),
            P("fsdp"),
            P("fsdp", None),
            P("fsdp", None),
        ),
        check_vma=False,
    )
```

```python
import functools

import jax
import jax.numpy as jnp
from jax import lax
from jax.experimental import pallas as pl
from jax.experimental.pallas import tpu as pltpu
from jax.sharding import PartitionSpec as P

HEADS = 16
HEAD_DIM = 64
BUCKETS = 32
T = 256
NEG = -1e30
F32 = jnp.float32
BF = jnp.bfloat16
GROUPS = 8
CHUNKS = 4
HEAD_GROUPS = 4
NN = (((1,), (0,)), ((), ()))
NT = (((1,), (1,)), ((), ()))
TN = (((0,), (0,)), ((), ()))
TT = (((0,), (1,)), ((), ()))
ANY = pl.BlockSpec(memory_space=pl.ANY)
SMEM = pl.BlockSpec(memory_space=pltpu.SMEM)


def dot(a, b, form=NN):
    return lax.dot_general(a, b, form, preferred_element_type=F32)


def params(mib=60):
    return pltpu.CompilerParams(vmem_limit_bytes=mib << 20)


def cost(flops, moved, exps=0):
    return pl.CostEstimate(flops=int(flops), bytes_accessed=int(moved), transcendentals=int(exps))


def resident(shape):
    return pl.BlockSpec(shape, lambda i, *_: (0,) * len(shape))


def shape_of(shape, kind):
    return jax.ShapeDtypeStruct(shape, kind)


def last_block(part, width):
    at = part.shape[1] // width - 1
    return pl.BlockSpec((part.shape[0], width), lambda i: (0, at))


def block_of(me, r):
    return pl.multiple_of(jnp.bitwise_xor(me, r) * 128, 128)


PLACES = ((0, 0, 1), (2, 0, 1), (4, 0, 1), (6, 0, 2), (6, 1, 2), (1, 0, 1), (3, 0, 1), (5, 0, 1), (7, 0, 2), (7, 1, 2))


def in_order(parts):
    by = {(r, half): p for (r, half, _), p in zip(PLACES, parts)}
    return [by[r, half] for r in range(8) for half in range(2 if r >= 6 else 1)]


def normalise(v):
    centred = v - jnp.mean(v, axis=-1, keepdims=True)
    rstd = lax.rsqrt(jnp.mean(centred * centred, axis=-1, keepdims=True) + 1e-5)
    return centred * rstd, rstd


def with_deps(kernel, inputs, count):
    def body(*refs):
        return kernel(*refs[:inputs], *refs[inputs + count:])
    return body


def prepare_kernel(me_ref, len_ref, x_ref, cot_ref, bucket_ref, *refs):
    small_ref, n1t_ref, og_ref, vec_ref, base_ref, abs_s = refs
    me = me_ref[0]
    rows = x_ref.shape[0]

    @pl.when(pl.program_id(0) == 0)
    def _():
        small = small_ref[...].astype(F32)
        for r in range(8):
            for k in range(4):
                vec_ref[k:k + 1, pl.ds(block_of(me, r), 128)] = small[r:r + 1, k * 128:(k + 1) * 128]
        table = jnp.concatenate([
            small[h // 2:h // 2 + 1, 512 + h % 2 * BUCKETS:512 + (h % 2 + 1) * BUCKETS] for h in range(HEADS)]).astype(BF)
        slots = bucket_ref.shape[1]
        onehot = (bucket_ref[...] == lax.broadcasted_iota(jnp.int32, (BUCKETS, slots), 0)).astype(BF)
        by = dot(table, onehot)
        for u in range(slots // T):
            base_ref[:, u, :] = by[:, slots - (u + 1) * T:slots - u * T]

    hat, _ = normalise(x_ref[...].astype(F32))
    abs_s[...] = hat * vec_ref[0:1] + vec_ref[1:2]
    for r in range(8):
        n1t_ref[r * 128:(r + 1) * 128, :] = abs_s[:, pl.ds(block_of(me, r), 128)].astype(BF).T
    slot = pl.program_id(0) * rows + lax.broadcasted_iota(jnp.int32, (rows, 1), 0)
    og_ref[...] = jnp.where(slot < len_ref[0], cot_ref[...], jnp.zeros_like(cot_ref))


def prepare(me, lengths, x, cot, buckets, small, deps=()):
    rows, width = x.shape
    tile = pl.BlockSpec((T, width), lambda i: (i, 0))
    return pl.pallas_call(
        with_deps(prepare_kernel, 6, len(deps)), grid=(rows // T,), name="prepare",
        in_specs=[SMEM, SMEM, tile, tile, resident(buckets.shape), resident(small.shape)] + [ANY] * len(deps),
        out_specs=[pl.BlockSpec((width, T), lambda i: (0, i)), tile, resident((4, width)), resident((HEADS, rows // T, T))],
        out_shape=[shape_of((width, rows), BF), shape_of((rows, width), BF), shape_of((4, width), F32),
                   shape_of((HEADS, rows // T, T), F32)],
        scratch_shapes=[pltpu.VMEM((T, width), F32)],
        compiler_params=params(), cost_estimate=cost(1e9, 8e6),
    )(me, lengths, x, cot, buckets, small, *deps)


def pack_kernel(wi_ref, wd_ref, *refs):
    for c, out in enumerate(refs):
        for k in range(2):
            for b in range(8):
                col = (b * CHUNKS + 2 * c + k) * 128
                out[k, :128, b * 128:(b + 1) * 128] = wi_ref[:, col:col + 128]
            out[k, 128:, :] = wd_ref[(2 * c + k) * 128:(2 * c + k + 1) * 128, :]


def pack(w_in, w_down, deps):
    vm = pl.BlockSpec(memory_space=pltpu.VMEM)
    return pl.pallas_call(
        with_deps(pack_kernel, 2, len(deps)), name="pack", in_specs=[vm] * 2 + [ANY] * len(deps), out_specs=[vm] * 2,
        out_shape=[shape_of((2, 256, 1024), BF)] * 2, compiler_params=params(), cost_estimate=cost(1e6, 4e6),
    )(w_in, w_down, *deps)


def lead_kernel(qkv_ref, out_ref, a_ref, b_ref, c_ref, d_ref, e_ref, piece_ref, small_ref):
    cols = qkv_ref.shape[1]
    piece_ref[:, :cols] = qkv_ref[...]
    piece_ref[:, cols:] = out_ref[...]
    at = 0
    for ref in (a_ref, b_ref, c_ref, d_ref, e_ref):
        small_ref[:, at:at + ref.shape[1]] = ref[...]
        at += ref.shape[1]


def lead(w_qkv, w_out, *small):
    vm = pl.BlockSpec(memory_space=pltpu.VMEM)
    rows, cols = w_qkv.shape[0], w_qkv.shape[1] + w_out.shape[1]
    small = [v[None] for v in small]
    return pl.pallas_call(
        lead_kernel, name="lead", in_specs=[vm] * 7, out_specs=[vm] * 2,
        out_shape=[shape_of((rows, cols), BF), shape_of((1, sum(v.shape[1] for v in small)), BF)],
        compiler_params=params(), cost_estimate=cost(1e6, 2e6),
    )(w_qkv, w_out, *small)


def project_kernel(n1t_ref, *refs):
    w = jnp.concatenate([r[...] for r in in_order(refs[:10])], axis=0)
    out = dot(w, n1t_ref[...], TN).astype(BF)
    refs[10][...] = out.reshape(refs[10].shape)


def project(n1t, parts):
    width, rows = n1t.shape
    cols = 3 * width
    tile = 512
    return pl.pallas_call(
        project_kernel, grid=(cols // tile,), name="project",
        in_specs=[resident((width, rows))] + [pl.BlockSpec((p.shape[0], tile), lambda i: (0, i)) for p in parts],
        out_specs=pl.BlockSpec((tile // HEAD_DIM, HEAD_DIM, rows), lambda i: (i, 0, 0)),
        out_shape=shape_of((cols // HEAD_DIM, HEAD_DIM, rows), BF),
        compiler_params=params(), cost_estimate=cost(2 * rows * width * cols, 14e6),
    )(n1t, *parts)


def toeplitz(base_ref):
    row = lax.broadcasted_iota(jnp.int32, (T, T), 0)
    col = lax.broadcasted_iota(jnp.int32, (T, T), 1)
    count = base_ref.shape[1]
    rolled = [
        pltpu.roll(jnp.broadcast_to(base_ref[0, u:u + 1, :], (T, T)), 0, 1, stride=1, stride_axis=0)
        for u in range(count)
    ]
    return [jnp.where(col >= row, rolled[u], rolled[u + 1] if u + 1 < count else NEG) for u in range(count)]


def key_mask(len_ref, start):
    slot = start + lax.broadcasted_iota(jnp.int32, (T, 1), 0)
    return jnp.where(slot < len_ref[0], 0.0, NEG).astype(F32)


def attend_kernel(me_ref, len_ref, base_ref, q_ref, k_ref, v_ref, o_ref, lt_ref, g_ref):
    tiles = base_ref.shape[1]
    for u, t in enumerate(toeplitz(base_ref)):
        g_ref[u * T:(u + 1) * T, :] = t
    k = k_ref[0].T
    v = v_ref[0]
    for b in range(tiles):
        nk = (b + 1) * T
        sl = slice(b * T, nk)
        q = q_ref[0, :, sl] * BF(HEAD_DIM ** -0.5)
        s = dot(k[:nk], q) + g_ref[(tiles - 1 - b) * T:, :]
        if b == tiles - 1:
            s = jnp.concatenate([s[:b * T], s[b * T:] + key_mask(len_ref, b * T)], axis=0)
        m = jnp.max(s, axis=0, keepdims=True)
        p = jnp.exp(s - m)
        total = jnp.sum(p, axis=0, keepdims=True)
        o = dot(v[:, :nk], p.astype(BF))
        o_ref[0, :, sl] = (o * (1.0 / total)).astype(BF)
        lt_ref[0, :, sl] = m + jnp.log(total)


def head_place(h, me_ref):
    return jnp.bitwise_xor(h // 2, me_ref[0]) * 2 + h % 2


def attend(me, lengths, base, qkv):
    heads = HEADS
    rows = qkv.shape[-1]
    tiles = rows // T
    block = (1, HEAD_DIM, rows)
    at = lambda off: pl.BlockSpec(block, lambda h, m: (h + off, 0, 0))
    return pl.pallas_call(
        attend_kernel, name="attend",
        grid_spec=pltpu.PrefetchScalarGridSpec(
            num_scalar_prefetch=1, grid=(heads,),
            in_specs=[SMEM, pl.BlockSpec((1, tiles, T), lambda h, m: (head_place(h, m), 0, 0)), at(0), at(heads), at(2 * heads)],
            out_specs=[pl.BlockSpec(block, lambda h, m: (head_place(h, m), 0, 0)),
                       pl.BlockSpec((1, 1, rows), lambda h, m: (h, 0, 0))],
            scratch_shapes=[pltpu.VMEM((rows, T), F32)]),
        out_shape=[shape_of((heads, HEAD_DIM, rows), BF), shape_of((heads, 1, rows), F32)],
        compiler_params=params(), cost_estimate=cost(30e9, 10e6),
    )(me, lengths, base, qkv, qkv, qkv)


def skew_sums(dg_ref, dist_ref):
    row = lax.broadcasted_iota(jnp.int32, (T, T), 0)
    col = lax.broadcasted_iota(jnp.int32, (T, T), 1)
    for u in range(dist_ref.shape[1]):
        z = jnp.where(col >= row, dg_ref[u * T:(u + 1) * T, :], dg_ref[(u - 1) * T:u * T, :] if u else 0.0)
        acc = z[0:8]
        for g in range(1, T // 8):
            acc = acc + pltpu.roll(z[8 * g:8 * g + 8], T - 8 * g, 1)
        tot = acc[0:1]
        for r in range(1, 8):
            tot = tot + pltpu.roll(acc[r:r + 1], T - r, 1)
        dist_ref[0, u:u + 1, :] = tot


def attend_back_kernel(me_ref, len_ref, base_ref, q_ref, k_ref, v_ref, o_ref, do_ref, lt_ref,
                       dq_ref, dk_ref, dv_ref, dist_ref, g_ref, dg_ref, dk_s, dv_s):
    tiles = base_ref.shape[1]
    scale = HEAD_DIM ** -0.5
    for u, t in enumerate(toeplitz(base_ref)):
        g_ref[u * T:(u + 1) * T, :] = t
    kt = k_ref[0]
    k = kt.T
    v = v_ref[0].T
    for b in range(tiles - 1, -1, -1):
        nk = (b + 1) * T
        sl = slice(b * T, nk)
        low = (tiles - 1 - b) * T
        q = q_ref[0, :, sl] * BF(scale)
        do = do_ref[0, :, sl]
        inner = jnp.sum(do.astype(F32) * o_ref[0, :, sl].astype(F32), axis=0, keepdims=True)
        s = dot(k[:nk], q) + g_ref[low:, :]
        if b == tiles - 1:
            s = jnp.concatenate([s[:b * T], s[b * T:] + key_mask(len_ref, b * T)], axis=0)
        p = jnp.exp(s - lt_ref[0, :, sl])
        ds = p * (dot(v[:nk], do) - inner)
        pb = p.astype(BF)
        dsb = ds.astype(BF)
        dq_ref[0, :, sl] = (dot(kt[:, :nk], dsb) * scale).astype(BF)
        dvp = dot(do, pb, NT)
        dkp = dot(q, dsb, NT)
        if b == tiles - 1:
            dk_s[...] = dkp
            dv_s[...] = dvp
            dg_ref[...] = ds
        else:
            dk_s[:, :nk] += dkp
            dv_s[:, :nk] += dvp
            dg_ref[low:, :] += ds
    dk_ref[0] = dk_s[...].astype(BF)
    dv_ref[0] = dv_s[...].astype(BF)
    skew_sums(dg_ref, dist_ref)


def attend_back(me, lengths, base, qkv, o, do, lt, first, count, deps=()):
    rows = qkv.shape[-1]
    tiles = rows // T
    block = (1, HEAD_DIM, rows)
    at = lambda off: pl.BlockSpec(block, lambda h, m: (h + off + first, 0, 0))
    placed = pl.BlockSpec(block, lambda h, m: (head_place(h + first, m), 0, 0))
    out = pl.BlockSpec(block, lambda h, m: (h, 0, 0))
    return pl.pallas_call(
        with_deps(attend_back_kernel, 9, len(deps)), name="attend_back",
        grid_spec=pltpu.PrefetchScalarGridSpec(
            num_scalar_prefetch=1, grid=(count,),
            in_specs=[SMEM, pl.BlockSpec((1, tiles, T), lambda h, m: (head_place(h + first, m), 0, 0)), at(0), at(HEADS), at(2 * HEADS),
                      placed, placed, pl.BlockSpec((1, 1, rows), lambda h, m: (h + first, 0, 0))] + [ANY] * len(deps),
            out_specs=[out, out, out, pl.BlockSpec((1, tiles, T), lambda h, m: (h, 0, 0))],
            scratch_shapes=[pltpu.VMEM((rows, T), F32), pltpu.VMEM((rows, T), F32),
                            pltpu.VMEM((HEAD_DIM, rows), F32), pltpu.VMEM((HEAD_DIM, rows), F32)]),
        out_shape=[shape_of((count, HEAD_DIM, rows), BF)] * 3 + [shape_of((count, tiles, T), F32)],
        compiler_params=params(), cost_estimate=cost(2.4e9 * count, 1.2e6 * count),
    )(me, lengths, base, qkv, qkv, qkv, o, do, lt, *deps)


def middle_kernel(me_ref, at_ref, x_ref, gain_ref, shift_ref, *refs):
    parts, (mid_ref, n2_ref, n2t_ref, abs_s) = refs[:10], refs[10:]
    me = me_ref[0]
    w = jnp.concatenate([r[...] for r in in_order(parts)], axis=0)
    mid = x_ref[...].astype(F32) + dot(at_ref[...], w, TN)
    mid_ref[...] = mid
    hat, _ = normalise(mid)
    abs_s[...] = hat * gain_ref[...] + shift_ref[...]
    for r in range(8):
        sl = slice(r * 128, (r + 1) * 128)
        part = abs_s[:, pl.ds(block_of(me, r), 128)].astype(BF)
        n2_ref[:, sl] = part
        n2t_ref[sl, :] = part.T


def middle_of(me, at, x, gain, shift, parts, deps=()):
    rows, width = x.shape
    tile = pl.BlockSpec((T, width), lambda i: (i, 0))
    turned = pl.BlockSpec((width, T), lambda i: (0, i))
    return pl.pallas_call(
        with_deps(middle_kernel, 5 + len(parts), len(deps)), grid=(rows // T,), name="middle",
        in_specs=[SMEM, turned, tile, resident((1, width)), resident((1, width))] + [last_block(p, width) for p in parts]
        + [ANY] * len(deps),
        out_specs=[tile, tile, turned],
        out_shape=[shape_of((rows, width), F32), shape_of((rows, width), BF), shape_of((width, rows), BF)],
        scratch_shapes=[pltpu.VMEM((T, width), F32)],
        compiler_params=params(), cost_estimate=cost(2 * rows * width * width, 14e6),
    )(me, at, x, gain, shift, *parts, *deps)


def gelu_parts(x):
    a = jnp.abs(x)
    t = 1.0 / (1.0 + a * (0.3275911 * 0.7071067811865476))
    e = jnp.exp(x * x * -0.5)
    poly = t * (0.127414796 + t * (-0.142248368 + t * (0.7107068705 + t * (-0.7265760135 + t * 0.5307027145))))
    q = poly * e
    phi = jnp.where(x >= 0.0, 1.0 - q, q)
    return x * phi, phi + x * (e * 0.3989422804014327)


def feed_kernel(c, stacked, counts, me_ref, n2_h, n2t_h, og_h, w_h, *refs):
    carried, held, deps, outs = counts
    carry, refs = refs[:carried], refs[carried + held + deps:]
    outs, refs = refs[:outs], refs[outs:]
    n2_v, n2t_v, og_v, w_v, y_v, g_v, send_v, keep_v, sem_in, sem_out = refs
    me = me_ref[0]
    loads = [(n2_h, n2_v)]
    loads += [(w_h.at[jnp.bitwise_xor(me, r), c], w_v.at[r]) for r in range(8)]
    loads += [(og_h, og_v)]
    early = len(loads)
    loads += list(zip(carry, (y_v, g_v))) + [(n2t_h, n2t_v)]
    copies = [pltpu.make_async_copy(a, b, sem_in.at[i]) for i, (a, b) in enumerate(loads)]
    for x in copies:
        x.start()
    for x in copies[:early]:
        x.wait()
    pairs = [(y_v, outs[0]), (g_v, outs[1])]
    if stacked:
        pairs += [((send_v if r % 2 else keep_v).at[r // 2], outs[2].at[jnp.bitwise_xor(me, r), c]) for r in range(8)]
    else:
        pairs += [(send_v, outs[2].at[:, c]), (keep_v, outs[3].at[:, c])]
    stores = [pltpu.make_async_copy(a, b, sem_out.at[i]) for i, (a, b) in enumerate(pairs)]
    n2 = n2_v[...]
    og = og_v[...]
    for t in range(2):
        offs = [block_of(me, 4 * t + j) for j in range(4)]
        wi = jnp.concatenate([w_v[:, :128, pl.ds(o, 128)].reshape(1024, 128) for o in offs], axis=1)
        wd = w_v[4 * t:4 * t + 4, 128:, :].reshape(512, 1024)
        hid, slope = gelu_parts(dot(n2, wi))
        hid = hid.astype(BF)
        pre = (dot(og, wd, NT) * slope).astype(BF)
        if t == 0:
            for x in copies[early:]:
                x.wait()
        if not carried and t == 0:
            y_v[...] = dot(hid, wd)
            g_v[...] = dot(pre, wi, NT)
        else:
            y_v[...] += dot(hid, wd)
            g_v[...] += dot(pre, wi, NT)
        if t == 1:
            stores[0].start()
            stores[1].start()
        dwi = dot(n2t_v[...], pre).astype(BF)
        for r in range(8):
            for j, o in enumerate(offs):
                (send_v if r % 2 else keep_v)[r // 2, :128, pl.ds(o, 128)] = dwi[r * 128:(r + 1) * 128, j * 128:(j + 1) * 128]
        dwd = dot(hid, og, TN).astype(BF)
        for j in range(4):
            r = 4 * t + j
            (send_v if r % 2 else keep_v)[r // 2, 128:, :] = dwd[j * 128:(j + 1) * 128]
    for x in stores[2:]:
        x.start()
    for x in stores:
        x.wait()


def feed(c, stacked, me, n2, n2t, og, w, carry, held, deps=()):
    rows, width = n2.shape
    half = (4, 256, 1024)
    carry = carry or ()
    grads = [(8, 2, 256, 1024)] if stacked else [(4, 2, 256, 1024)] * 2
    counts = (len(carry), len(held), len(deps), 2 + len(grads))
    n_in = 11 + len(carry)
    n_out = 10 if stacked else 4
    return pl.pallas_call(
        functools.partial(feed_kernel, c, stacked, counts), name="feed",
        in_specs=[SMEM] + [ANY] * (4 + sum(counts[:3])), out_specs=[ANY] * counts[3],
        out_shape=[shape_of((rows, width), F32)] * 2 + [shape_of(g, BF) for g in grads],
        input_output_aliases={5 + len(carry) + i: 2 + i for i in range(len(held))},
        scratch_shapes=[pltpu.VMEM((rows, width), BF), pltpu.VMEM((width, rows), BF), pltpu.VMEM((rows, width), BF),
                        pltpu.VMEM((8, 256, 1024), BF), pltpu.VMEM((rows, width), F32), pltpu.VMEM((rows, width), F32),
                        pltpu.VMEM(half, BF), pltpu.VMEM(half, BF),
                        pltpu.SemaphoreType.DMA((n_in,)), pltpu.SemaphoreType.DMA((n_out,))],
        compiler_params=params(), cost_estimate=cost(20e9, 30e6),
    )(me, n2, n2t, og, w, *carry, *held, *deps)


def norm_back(hat, rstd, grad, gain):
    t = grad * gain
    return (t - jnp.mean(t, axis=-1, keepdims=True) - hat * jnp.mean(t * hat, axis=-1, keepdims=True)) * rstd


def middle_back_kernel(me_ref, mid_ref, g_ref, og_ref, at_ref, gain_ref, *refs):
    parts, (mg_ref, do_ref, send_ref, keep_ref, vec_ref, abs_s, acc_s) = refs[:10], refs[10:]
    me = me_ref[0]
    i = pl.program_id(0)
    for r in range(8):
        abs_s[:, pl.ds(block_of(me, r), 128)] = g_ref[:, r * 128:(r + 1) * 128]
    grad = abs_s[...]
    hat, rstd = normalise(mid_ref[...])
    sums = jnp.concatenate([jnp.sum(grad * hat, axis=0, keepdims=True), jnp.sum(grad, axis=0, keepdims=True)], axis=0)
    mg = og_ref[...].astype(F32) + norm_back(hat, rstd, grad, gain_ref[...])
    mg_ref[...] = mg
    branch = mg.astype(BF)
    w = jnp.concatenate([r[...] for r in in_order(parts)], axis=0)
    do_ref[...] = dot(w, branch, NT).astype(BF)
    dw = dot(at_ref[...], branch)

    @pl.when(i == 0)
    def _():
        vec_ref[...] = sums
        acc_s[...] = dw

    @pl.when(i > 0)
    def _():
        vec_ref[...] += sums
        acc_s[...] += dw

    @pl.when(i == pl.num_programs(0) - 1)
    def _():
        for r in range(8):
            (send_ref if r % 2 else keep_ref)[r // 2] = acc_s[r * 128:(r + 1) * 128, :].astype(BF)


def middle_back(me, mid, g, og, at, gain, parts, deps=()):
    rows, width = mid.shape
    tile = pl.BlockSpec((T, width), lambda i: (i, 0))
    turned = pl.BlockSpec((width, T), lambda i: (0, i))
    block = (4, 128, width)
    return pl.pallas_call(
        with_deps(middle_back_kernel, 6 + len(parts), len(deps)), grid=(rows // T,), name="middle_back",
        in_specs=[SMEM, tile, tile, tile, turned, resident((1, width))] + [last_block(p, width) for p in parts] + [ANY] * len(deps),
        out_specs=[tile, turned, resident(block), resident(block), resident((2, width))],
        out_shape=[shape_of((rows, width), F32), shape_of((width, rows), BF), shape_of(block, BF), shape_of(block, BF),
                   shape_of((2, width), F32)],
        scratch_shapes=[pltpu.VMEM((T, width), F32), pltpu.VMEM((width, width), F32)],
        compiler_params=params(), cost_estimate=cost(4 * rows * width * width, 24e6),
    )(me, mid, g, og, at, gain, *parts, *deps)


def staged_kernel(steps, count, deps, where_ref, *refs):
    n_out = sum(len(outs) for _, outs, _ in steps)
    sources, refs = refs[:count], refs[count + deps:]
    dests, refs = refs[:n_out], refs[n_out:]
    held, kept, sem_in, sem_out = refs[:count], refs[count:count + n_out], refs[-2], refs[-1]
    loads = []
    for ins, _, _ in steps:
        for _, index in ins:
            k = len(loads)
            loads.append(pltpu.make_async_copy(sources[k].at[index] if index else sources[k], held[k], sem_in.at[k]))
    for c in loads:
        c.start()
    stores = []
    a = b = 0
    for ins, outs, fn in steps:
        for c in loads[a:a + len(ins)]:
            c.wait()
        fn(where_ref, held[a:a + len(ins)], kept[b:b + len(outs)])
        for k in range(b, b + len(outs)):
            stores.append(pltpu.make_async_copy(kept[k], dests[k], sem_out.at[k]))
            stores[-1].start()
        a += len(ins)
        b += len(outs)
    for c in stores:
        c.wait()


def staged(where, steps, deps=()):
    steps = [([v if isinstance(v, tuple) else (v, ()) for v in ins], outs, fn) for ins, outs, fn in steps]
    arrays = [v for ins, _, _ in steps for v, _ in ins]
    held = [shape_of(v.shape[len(index):], v.dtype) for ins, _, _ in steps for v, index in ins]
    outs = [o for _, outs, _ in steps for o in outs]
    flat = pl.pallas_call(
        functools.partial(staged_kernel, steps, len(arrays), len(deps)), name="staged",
        in_specs=[SMEM] + [ANY] * (len(arrays) + len(deps)), out_specs=[ANY] * len(outs), out_shape=outs,
        scratch_shapes=[pltpu.VMEM(v.shape, v.dtype) for v in held + outs]
        + [pltpu.SemaphoreType.DMA((len(arrays),)), pltpu.SemaphoreType.DMA((len(outs),))],
        compiler_params=params(), cost_estimate=cost(3e9, 10e6),
    )(where, *arrays, *deps)
    result = []
    for _, o, _ in steps:
        result.append(flat[:len(o)])
        flat = flat[len(o):]
    return result


def plus(*refs):
    total = refs[0].astype(F32)
    for r in refs[1:]:
        total = total + r.astype(F32)
    return total


def project_back(n1t, three, extra=()):
    cols = three[0].shape[0]
    before = sum(e[0].shape[2] for e in extra)
    block = shape_of((4, 128, before + 3 * cols), BF)

    def fn(_, ins, outs):
        at = 0
        for k in range(len(extra)):
            width = ins[4 + 2 * k].shape[2]
            outs[0][:, :, at:at + width] = ins[4 + 2 * k][...]
            outs[1][:, :, at:at + width] = ins[5 + 2 * k][...]
            at += width
        n1 = ins[0][...]
        for j in range(3):
            dw = dot(n1, ins[1 + j][...], NT).astype(BF)
            for r in range(8):
                outs[r % 2 == 0][r // 2, :, at + j * cols:at + (j + 1) * cols] = dw[r * 128:(r + 1) * 128]

    return [n1t, *three] + [v for e in extra for v in e], [block, block], fn


def finish_kernel(groups, me_ref, len_ref, x_ref, mid_ref, y_ref, mg_ref, gain_ref, *refs):
    parts, refs = refs[:10], refs[10:]
    grads, (out_ref, ig_ref, vec_ref, abs_s) = refs[:3 * groups], refs[3 * groups:]
    me = me_ref[0]
    i = pl.program_id(0)
    rows, width = x_ref.shape
    w = jnp.concatenate([r[...] for r in in_order(parts)], axis=0)
    total = jnp.zeros((rows, width), F32)
    pg = jnp.concatenate([grads[3 * g + j][...] for j in range(3) for g in range(groups)], axis=0)
    total = dot(pg, w, TT)
    for r in range(8):
        abs_s[:, pl.ds(block_of(me, r), 128)] = total[:, r * 128:(r + 1) * 128]
    grad = abs_s[...]
    hat, rstd = normalise(x_ref[...].astype(F32))
    sums = jnp.concatenate([jnp.sum(grad * hat, axis=0, keepdims=True), jnp.sum(grad, axis=0, keepdims=True)], axis=0)
    ig_ref[...] = mg_ref[...] + norm_back(hat, rstd, grad, gain_ref[...])
    slot = i * rows + lax.broadcasted_iota(jnp.int32, (rows, 1), 0)
    out_ref[...] = jnp.where(slot < len_ref[0], mid_ref[...] + y_ref[...], 0.0).astype(BF)

    @pl.when(i == 0)
    def _():
        vec_ref[...] = sums

    @pl.when(i > 0)
    def _():
        vec_ref[...] += sums


def finish(me, lengths, x, mid, y, mg, gain, parts, grads, deps=()):
    rows, width = x.shape
    tile = pl.BlockSpec((T, width), lambda i: (i, 0))
    return pl.pallas_call(
        with_deps(functools.partial(finish_kernel, len(grads) // 3), 7 + len(parts) + len(grads), len(deps)),
        grid=(rows // T,), name="finish",
        in_specs=[SMEM, SMEM, tile, tile, tile, tile, resident((1, width))] + [resident((p.shape[0], 3 * width)) for p in parts]
        + [pl.BlockSpec((g.shape[0], T), lambda i: (0, i)) for g in grads] + [ANY] * len(deps),
        out_specs=[tile, tile, resident((2, width))],
        out_shape=[shape_of((rows, width), BF), shape_of((rows, width), F32), shape_of((2, width), F32)],
        scratch_shapes=[pltpu.VMEM((T, width), F32)],
        compiler_params=params(), cost_estimate=cost(6 * rows * width * width, 34e6),
    )(me, lengths, x, mid, y, mg, gain, *parts, *grads, *deps)


def flip(v, k):
    return lax.ppermute(v, "fsdp", [(i, i ^ k) for i in range(GROUPS)])


def xor_rows(v, me):
    for k in (1, 2, 4):
        turned = v.reshape((8 // (2 * k), 2, k) + v.shape[1:])[:, ::-1].reshape(v.shape)
        v = jnp.where((me & k) != 0, turned, v)
    return v


def split_full(full):
    m = full.shape[0] // 8
    return [full[r * m + half * (m // of):r * m + (half + 1) * (m // of)] for r, half, of in PLACES]


def add(*vs):
    total = vs[0].astype(F32)
    for v in vs[1:]:
        total = total + v.astype(F32)
    return total.astype(vs[0].dtype)


def scatter_sums(keep, got):
    h, c = keep.shape[1] // 2, keep.shape[2]

    def fn(_, ins, outs):
        k, g = ins
        for out, half, pair in zip(outs, (0, 1, 0, 1), ((1, 3), (2, 3), (0, 2), (0, 1))):
            for n, j in enumerate(pair):
                out[n] = plus(k[j, half * h:(half + 1) * h, :], g[j, half * h:(half + 1) * h, :]).astype(BF)

    return [keep, got], [shape_of((2, h, c), BF)] * 4, fn


def scatter_second(sums, ga, gb):
    def fn(_, ins, outs):
        outs[0][...] = plus(ins[0][...], ins[1][...]).astype(BF)
        outs[1][...] = plus(ins[2][...], ins[3][...]).astype(BF)

    return [(sums[2], (1,)), (ga, (1,)), (sums[3], (1,)), (gb, (1,))], [shape_of(sums[2].shape[1:], BF)] * 2, fn


def scatter_last(sums, ga, gb, fa, fb, split):
    h, c = fa.shape

    def fn(where, ins, outs):
        a = plus(ins[0][...], ins[1][...], ins[2][...]).astype(BF)
        b = plus(ins[3][...], ins[4][...], ins[5][...]).astype(BF)
        if split:
            odd = where[1] == 1
            outs[0][...] = jnp.where(odd, a, b)
            outs[1][...] = jnp.where(odd, b, a)
        else:
            outs[0][:h] = a
            outs[0][h:] = b

    out = [shape_of((h, c), BF)] * 2 if split else [shape_of((2 * h, c), BF)]
    return [(sums[2], (0,)), (ga, (0,)), fa, (sums[3], (0,)), (gb, (0,)), fb], out, fn


def copies_second(keep, got):
    q, c = keep.shape[0] // 2, keep.shape[1]

    def fn(where, ins, outs):
        a = plus(ins[0][:q], ins[1][:q]).astype(BF)
        b = plus(ins[0][q:], ins[1][q:]).astype(BF)
        high = where[2] == 1
        outs[0][...] = jnp.where(high, a, b)
        outs[1][...] = jnp.where(high, b, a)

    return [keep, got], [shape_of((q, c), BF)] * 2, fn


def copies_third(keep, got):
    def fn(_, ins, outs):
        outs[0][...] = plus(ins[0][...], ins[1][...]).astype(BF)

    return [keep, got], [shape_of(keep.shape, BF)], fn


def copies_join(mine, got, bit):
    q, c = mine.shape

    def fn(where, ins, outs):
        second = where[bit] == 1
        a, b = ins[0][...], ins[1][...]
        outs[0][:q] = jnp.where(second, b, a)
        outs[0][q:] = jnp.where(second, a, b)

    return [mine, got], [shape_of((2 * q, c), BF)], fn


def vector_sums(where, vec_one, vec_two, dists, buckets):
    def fn(where, ins, outs):
        by = jnp.concatenate([jnp.concatenate([d[:, u, :] for u in range(d.shape[1] - 1, -1, -1)], axis=1) for d in ins[2:-1]])
        onehot = (ins[-1][...] == lax.broadcasted_iota(jnp.int32, (BUCKETS, by.shape[1]), 0)).astype(F32)
        table = lax.dot_general(by, onehot, NT, precision=lax.Precision.HIGHEST, preferred_element_type=F32)
        outs[2][...] = jnp.concatenate([jnp.concatenate([table[2 * r:2 * r + 1], table[2 * r + 1:2 * r + 2]], axis=1) for r in range(8)])
        for r in range(8):
            out = outs[1 - r % 2]
            row = slice(r // 2, r // 2 + 1)
            for k in range(4):
                out[row, k * 128:(k + 1) * 128] = ins[k // 2][k % 2:k % 2 + 1, pl.ds(block_of(where[0], r), 128)]
            out[row, 512:] = outs[2][pl.ds(jnp.bitwise_xor(where[0], r), 1), :]

    out = shape_of((4, 576), F32)
    return [vec_one, vec_two, *dists, buckets], [out, out, shape_of((8, 64), F32)], fn


def vector_halve(keep, got):
    n = keep.shape[0] // 2

    def fn(_, ins, outs):
        for k in range(n):
            for out, row in zip(outs, (2 * k + 1, 2 * k)):
                out[k:k + 1] = ins[0][row:row + 1] + ins[1][row:row + 1]

    return [keep, got], [shape_of((n, 576), F32)] * 2, fn


def vector_add(*vs):
    def fn(_, ins, outs):
        outs[0][...] = plus(*(r[...] for r in ins))

    return list(vs), [shape_of(vs[0].shape, F32)], fn


def feed_result(one, two):
    def fn(_, ins, outs):
        for c in range(CHUNKS):
            v = ins[c // 2]
            base = c % 2 * 256
            for b in range(8):
                col = (b * CHUNKS + c) * 128
                outs[0][:, col:col + 128] = v[base:base + 128, b * 128:(b + 1) * 128].astype(F32)
            outs[1][c * 128:(c + 1) * 128, :] = v[base + 128:base + 256, :].astype(F32)

    return [one, two], [shape_of((128, 4096), F32), shape_of((512, 1024), F32)], fn


def project_result(v1, v3, x3, v4, x4):
    def fn(where, ins, outs):
        qkv, out = outs
        v1, v3, x3, *v4 = ins
        width = out.shape[1]
        part = qkv.shape[1] // (3 * HEAD_GROUPS)
        out[...] = v1[:, :width].astype(F32)
        odd = where[1] == 1
        a, b = v3[...], x3[...]
        both = jnp.concatenate([jnp.where(odd, b, a), jnp.where(odd, a, b)]).astype(F32)
        last = plus(*(r[...] for r in v4)).astype(BF).astype(F32)
        for j in range(3):
            base = j * HEAD_GROUPS * part
            qkv[:, base:base + part] = v1[:, width + j * part:width + (j + 1) * part].astype(F32)
            for g in range(2):
                at = (3 * g + j) * part
                qkv[:, base + (g + 1) * part:base + (g + 2) * part] = both[:, at:at + part]
            qkv[:, base + 3 * part:base + 4 * part] = last[:, j * part:(j + 1) * part]

    return [v1, v3, x3, v4, *x4], [shape_of((128, 3072), F32), shape_of((128, 1024), F32)], fn


def copy_swap(v, k):
    return lax.ppermute(v, "rep", [(i, i ^ k) for i in range(4)])


def copy_turns(v, count):
    return [lax.ppermute(v, "rep", [(i, (i + k) % count) for i in range(count)]) for k in range(1, count)]


def copies_sum_flat(v, count):
    return add(v, *(lax.ppermute(v, "rep", [(i, (i + k) % count) for i in range(count)]) for k in range(1, count)))


def per_device(n_fsdp, n_rep, inputs, lengths, bucket_table, ln1_gain, ln1_shift, w_qkv, rel_bias, w_out, ln2_gain, ln2_shift,
               w_in, w_down, cotangent):
    near = n_fsdp == GROUPS and n_rep == 4
    _, slots, width = inputs.shape
    hidden = w_in.shape[1]
    me = lax.axis_index("fsdp").astype(jnp.int32) if near else jnp.int32(0)
    me1 = me.reshape(1)
    x = inputs.reshape(slots, width)
    cot = cotangent.reshape(slots, width)
    full = lambda w: lax.all_gather(w, "fsdp", axis=0, tiled=True)

    if near:
        piece, small = lead(w_qkv, w_out, ln1_gain, ln1_shift, ln2_gain, ln2_shift, rel_bias)
        half = piece.shape[0] // 2
        r2, r4 = flip(piece, 2), flip(piece, 4)
        for k in (1, 2, 4):
            small = jnp.concatenate([small, flip(small, k)])
        n1t, og, vecs, base = prepare(me1, lengths, x, cot, bucket_table[None], small, (r2, r4))
        r6a, r6b = flip(r2[:half], 4), flip(r4[half:], 2)
        ffn_w = [full(v.reshape(512, 1024)).reshape(8, 2, 256, 1024) for v in pack(w_in, w_down, (r2, r4, n1t))]
        parts = [piece, r2, r4, r6a, r6b]
        parts = parts + [flip(v, 1) for v in parts]
    else:
        n = ln1_gain.shape[0]
        small = full(jnp.concatenate([ln1_gain, ln1_shift, ln2_gain, ln2_shift, rel_bias])[None])
        small = jnp.concatenate([small[:, i * n:(i + 1) * n].reshape(8, 128) for i in range(4)] + [small[:, 4 * n:].reshape(8, 64)], axis=1)
        n1t, og, vecs, base = prepare(me1, lengths, x, cot, bucket_table[None], small)
        parts = split_full(jnp.concatenate([full(w_qkv), full(w_out)], axis=1))
        wi_c = full(w_in).reshape(8, width // 8, 8, CHUNKS, 128)
        wd_c = full(w_down).reshape(8, CHUNKS, 128, width)
        chunk = [jnp.concatenate([wi_c[:, :, :, c].reshape(8, width // 8, 1024), wd_c[:, c]], axis=1) for c in range(CHUNKS)]
        ffn_w = [jnp.stack(chunk[2 * h:2 * h + 2], axis=1) for h in range(2)]
    n = ln1_gain.shape[0]
    gain_one, shift_one, gain_two, shift_two = (vecs[i:i + 1] for i in range(4))
    qkv = project(n1t, parts)
    o, lt = attend(me1, lengths, base, qkv)
    at = o.reshape(width, slots)
    mid, n2, n2t = middle_of(me1, at, x, gain_two, shift_two, parts)
    y, g, one = feed(0, True, me1, n2, n2t, og, ffn_w[0], (), ())
    y, g, one = feed(1, True, me1, n2, n2t, og, ffn_w[0], (y, g), (one,))
    y, g, *two = feed(0, not near, me1, n2, n2t, og, ffn_w[1], (y, g), ())
    y, g, *two = feed(1, not near, me1, n2, n2t, og, ffn_w[1], (y, g), two)
    mg, do, out_send, out_keep, vec_two = middle_back(me1, mid, g, og, at, gain_two, parts)
    do = do.reshape(HEADS, HEAD_DIM, slots)
    per = HEADS // HEAD_GROUPS
    grads, dists = [], []
    rep = lax.axis_index("rep").astype(jnp.int32)
    where = jnp.stack([me, rep % 2, rep // 2])

    def back(k, deps=()):
        *three, dist = attend_back(me1, lengths, base, qkv, o, do, lt, k * per, per, deps)
        three = [v.reshape(per * HEAD_DIM, slots) for v in three]
        grads.extend(three)
        dists.append(dist)
        return three

    if near:
        h1 = lax.psum_scatter(one.reshape(8 * 512, 1024), "fsdp", scatter_dimension=0, tiled=True)
        send2, keep2 = (v.reshape(4, 512, 1024) for v in two)
        got2 = flip(send2, 1)
        (s2,) = staged(where, [scatter_sums(keep2, got2)], (mg,))
        g2 = flip(s2[0], 2), flip(s2[1], 4)
        t0 = back(0, s2)
        ((send1, keep1),) = staged(where, [project_back(n1t, t0, [(out_send, out_keep)])], (h1,))
        h1 = lax.psum(h1, "rep")
        got1 = flip(send1, 1)
        t1 = back(1, (send1,))
        p1, f2, s1 = staged(where, [project_back(n1t, t1), scatter_second(s2, *g2), scatter_sums(keep1, got1)])
        f2 = flip(f2[0], 4), flip(f2[1], 2)
        g1 = flip(s1[0], 2), flip(s1[1], 4)
        t2 = back(2, s1)
        (send3, keep3), c2, f1 = staged(where, [project_back(n1t, t2, [p1]), scatter_last(s2, *g2, *f2, True), scatter_second(s1, *g1)])
        got3 = flip(send3, 1)
        x2 = copy_swap(c2[0], 1)
        f1 = flip(f1[0], 4), flip(f1[1], 2)
        t3 = back(3, (send3,))
        (send4, keep4), c2, c1, s3 = staged(where, [
            project_back(n1t, t3), copies_second(c2[1], x2), scatter_last(s1, *g1, *f1, True), scatter_sums(keep3, got3)])
        got4 = flip(send4, 1)
        x2 = copy_swap(c2[0], 2)
        x1 = copy_swap(c1[0], 1)
        g3 = flip(s3[0], 2), flip(s3[1], 4)
        tail = (send4,)
    else:
        pieces = [staged(where, [project_back(n1t, back(k))])[0] for k in range(HEAD_GROUPS)]
        tail = ()
    outputs, input_grad, vec_one = finish(me1, lengths, x, mid, y, mg, gain_one, parts, grads, tail)

    if near:
        (out_v, keep_v, _), s4, (v2,), c1, f3 = staged(where, [
            vector_sums(where, vec_one, vec_two, dists, bucket_table[None]),
            scatter_sums(keep4, got4), copies_third(c2[1], x2), copies_second(c1[1], x1), scatter_second(s3, *g3)], (h1,))
        got_v = flip(out_v, 1)
        g4 = flip(s4[0], 2), flip(s4[1], 4)
        x2 = copy_swap(v2, 2)
        x1 = copy_swap(c1[0], 2)
        f3 = flip(f3[0], 4), flip(f3[1], 2)
        (out_v, keep_v), f4, (v2,), (v1,), c3 = staged(where, [
            vector_halve(keep_v, got_v),
            scatter_second(s4, *g4), copies_join(v2, x2, 2), copies_third(c1[1], x1), scatter_last(s3, *g3, *f3, True)])
        f4 = flip(f4[0], 4), flip(f4[1], 2)
        x2 = copy_swap(v2, 1)
        x1 = copy_swap(v1, 2)
        x3 = copy_swap(c3[0], 1)
        got_v = flip(out_v, 2)
        (out_v, keep_v), (v4,), (h2,), (v1,), c3 = staged(where, [
            vector_halve(keep_v, got_v),
            scatter_last(s4, *g4, *f4, False), copies_join(v2, x2, 1), copies_join(v1, x1, 2), copies_second(c3[1], x3)])
        x4 = copy_turns(v4, 4)
        got_v = flip(out_v, 4)
        x1 = copy_swap(v1, 1)
        x3 = copy_swap(c3[0], 2)
        (vec,), (v1,), (v3,), (in_grad, down_grad) = staged(where, [
            vector_add(keep_v, got_v), copies_join(v1, x1, 1), copies_third(c3[1], x3), feed_result(h1, h2)])
        got_v = copy_turns(vec, 4)
        x3 = copy_swap(v3, 2)
        (v3,), (tiny,) = staged(where, [copies_join(v3, x3, 2), vector_add(vec, *got_v)])
        x3 = copy_swap(v3, 1)
        ((qkv_grad, out_g),) = staged(where, [project_result(v1, v3, x3, v4, x4)])
        tiny = tiny[0]
    else:
        onehot = (bucket_table[:, None] == lax.iota(jnp.int32, BUCKETS)[None, :]).astype(F32)
        distance_total = jnp.concatenate(dists)[:, ::-1].reshape(HEADS, slots)
        table_grad = jnp.dot(distance_total, onehot, precision=lax.Precision.HIGHEST, preferred_element_type=F32)
        vec = jnp.concatenate([v.reshape(n_fsdp, -1) for v in (vec_one[0], vec_one[1], vec_two[0], vec_two[1], table_grad)], axis=1)
        reduced = lambda v: lax.psum(lax.psum_scatter(v, "fsdp", scatter_dimension=0, tiled=True), "rep")
        whole = lambda s, k: jnp.stack([k, s], axis=1).reshape((8,) + s.shape[1:])
        tiny = reduced(vec)[0]
        stack = jnp.concatenate([one, two[0]], axis=1)
        in_grad = reduced(stack[:, :, :128].reshape(8, CHUNKS, 128, 8, 128).transpose(0, 2, 3, 1, 4).reshape(width, hidden))
        down_grad = reduced(stack[:, :, 128:].reshape(hidden, width))
        out_g = reduced(whole(out_send, out_keep).reshape(width, width))
        qkv_grad = reduced(jnp.stack([whole(s, k).reshape(width, 3, -1) for s, k in pieces], axis=2).reshape(width, 3 * width))
    return (outputs.reshape(inputs.shape), input_grad.reshape(inputs.shape), tiny[:n], tiny[n:2 * n], qkv_grad.astype(F32),
            tiny[4 * n:], out_g.astype(F32), tiny[2 * n:3 * n], tiny[3 * n:4 * n], in_grad.astype(F32), down_grad.astype(F32))


def solution(mesh):
    rows = P(("rep", "fsdp"), None, None)
    vec = P("fsdp")
    mat = P("fsdp", None)
    return jax.shard_map(
        functools.partial(per_device, mesh.shape["fsdp"], mesh.shape["rep"]),
        mesh=mesh,
        in_specs=(rows, P(("rep", "fsdp")), P(), vec, vec, mat, vec, mat, vec, vec, mat, mat, rows),
        out_specs=(rows, rows, vec, vec, mat, vec, mat, vec, vec, mat, mat),
        check_vma=False,
    )
```

```python
import functools

import jax
import jax.numpy as jnp
from jax import lax
from jax.experimental import pallas as pl
from jax.experimental.pallas import tpu as pltpu
from jax.sharding import PartitionSpec as P

HEADS = 16
HEAD_DIM = 64
BUCKETS = 32
T = 256
NEG = -1e30
F32 = jnp.float32
BF = jnp.bfloat16
GROUPS = 8
CHUNKS = 4
HEAD_GROUPS = 4
NN = (((1,), (0,)), ((), ()))
NT = (((1,), (1,)), ((), ()))
TN = (((0,), (0,)), ((), ()))
TT = (((0,), (1,)), ((), ()))
ANY = pl.BlockSpec(memory_space=pl.ANY)
SMEM = pl.BlockSpec(memory_space=pltpu.SMEM)


def dot(a, b, form=NN):
    return lax.dot_general(a, b, form, preferred_element_type=F32)


def params(mib=60):
    return pltpu.CompilerParams(vmem_limit_bytes=mib << 20)


def cost(flops, moved, exps=0):
    return pl.CostEstimate(flops=int(flops), bytes_accessed=int(moved), transcendentals=int(exps))


def resident(shape):
    return pl.BlockSpec(shape, lambda i, *_: (0,) * len(shape))


def shape_of(shape, kind):
    return jax.ShapeDtypeStruct(shape, kind)


def last_block(part, width):
    at = part.shape[1] // width - 1
    return pl.BlockSpec((part.shape[0], width), lambda i: (0, at))


def block_of(me, r):
    return pl.multiple_of(jnp.bitwise_xor(me, r) * 128, 128)


PLACES = (0, 2, 4, 6, 1, 3, 5, 7)


def in_order(parts):
    return [parts[PLACES.index(r)] for r in range(8)]


def normalise(v):
    centred = v - jnp.mean(v, axis=-1, keepdims=True)
    rstd = lax.rsqrt(jnp.mean(centred * centred, axis=-1, keepdims=True) + 1e-5)
    return centred * rstd, rstd


def with_deps(kernel, inputs, count):
    def body(*refs):
        return kernel(*refs[:inputs], *refs[inputs + count:])
    return body


def prepare_kernel(me_ref, len_ref, x_ref, cot_ref, bucket_ref, *refs):
    small_ref, n1t_ref, og_ref, vec_ref, base_ref, abs_s = refs
    me = me_ref[0]
    rows = x_ref.shape[0]

    @pl.when(pl.program_id(0) == 0)
    def _():
        small = small_ref[...].astype(F32)
        for r in range(8):
            for k in range(4):
                vec_ref[k:k + 1, pl.ds(block_of(me, r), 128)] = small[r:r + 1, k * 128:(k + 1) * 128]
        table = jnp.concatenate([
            small[h // 2:h // 2 + 1, 512 + h % 2 * BUCKETS:512 + (h % 2 + 1) * BUCKETS] for h in range(HEADS)]).astype(BF)
        slots = bucket_ref.shape[1]
        onehot = (bucket_ref[...] == lax.broadcasted_iota(jnp.int32, (BUCKETS, slots), 0)).astype(BF)
        by = dot(table, onehot)
        for u in range(slots // T):
            base_ref[:, u, :] = by[:, slots - (u + 1) * T:slots - u * T]

    hat, _ = normalise(x_ref[...].astype(F32))
    abs_s[...] = hat * vec_ref[0:1] + vec_ref[1:2]
    for r in range(8):
        n1t_ref[r * 128:(r + 1) * 128, :] = abs_s[:, pl.ds(block_of(me, r), 128)].astype(BF).T
    slot = pl.program_id(0) * rows + lax.broadcasted_iota(jnp.int32, (rows, 1), 0)
    og_ref[...] = jnp.where(slot < len_ref[0], cot_ref[...], jnp.zeros_like(cot_ref))


def prepare(me, lengths, x, cot, buckets, small, deps=()):
    rows, width = x.shape
    tile = pl.BlockSpec((T, width), lambda i: (i, 0))
    return pl.pallas_call(
        with_deps(prepare_kernel, 6, len(deps)), grid=(rows // T,), name="prepare",
        in_specs=[SMEM, SMEM, tile, tile, resident(buckets.shape), resident(small.shape)] + [ANY] * len(deps),
        out_specs=[pl.BlockSpec((width, T), lambda i: (0, i)), tile, resident((4, width)), resident((HEADS, rows // T, T))],
        out_shape=[shape_of((width, rows), BF), shape_of((rows, width), BF), shape_of((4, width), F32),
                   shape_of((HEADS, rows // T, T), F32)],
        scratch_shapes=[pltpu.VMEM((T, width), F32)],
        compiler_params=params(), cost_estimate=cost(1e9, 8e6),
    )(me, lengths, x, cot, buckets, small, *deps)


def pack_kernel(wi_ref, wd_ref, *refs):
    for c, out in enumerate(refs):
        for k in range(2):
            for b in range(8):
                col = (b * CHUNKS + 2 * c + k) * 128
                out[k, :128, b * 128:(b + 1) * 128] = wi_ref[:, col:col + 128]
            out[k, 128:, :] = wd_ref[(2 * c + k) * 128:(2 * c + k + 1) * 128, :]


def pack(w_in, w_down, deps):
    vm = pl.BlockSpec(memory_space=pltpu.VMEM)
    return pl.pallas_call(
        with_deps(pack_kernel, 2, len(deps)), name="pack", in_specs=[vm] * 2 + [ANY] * len(deps), out_specs=[vm] * 2,
        out_shape=[shape_of((2, 256, 1024), BF)] * 2, compiler_params=params(), cost_estimate=cost(1e6, 4e6),
    )(w_in, w_down, *deps)


def lead_kernel(qkv_ref, out_ref, a_ref, b_ref, c_ref, d_ref, e_ref, piece_ref, small_ref):
    cols = qkv_ref.shape[1]
    piece_ref[:, :cols] = qkv_ref[...]
    piece_ref[:, cols:] = out_ref[...]
    at = 0
    for ref in (a_ref, b_ref, c_ref, d_ref, e_ref):
        small_ref[:, at:at + ref.shape[1]] = ref[...]
        at += ref.shape[1]


def lead(w_qkv, w_out, *small):
    vm = pl.BlockSpec(memory_space=pltpu.VMEM)
    rows, cols = w_qkv.shape[0], w_qkv.shape[1] + w_out.shape[1]
    small = [v[None] for v in small]
    return pl.pallas_call(
        lead_kernel, name="lead", in_specs=[vm] * 7, out_specs=[vm] * 2,
        out_shape=[shape_of((rows, cols), BF), shape_of((1, sum(v.shape[1] for v in small)), BF)],
        compiler_params=params(), cost_estimate=cost(1e6, 2e6),
    )(w_qkv, w_out, *small)


def halves_kernel(a_ref, b_ref, a_out, b_out):
    half = a_out.shape[0]
    a_out[...] = a_ref[:half]
    b_out[...] = b_ref[half:]


def halves(a, b):
    vm = pl.BlockSpec(memory_space=pltpu.VMEM)
    out = shape_of((a.shape[0] // 2, a.shape[1]), a.dtype)
    return pl.pallas_call(
        halves_kernel, name="halves", in_specs=[vm] * 2, out_specs=[vm] * 2, out_shape=[out] * 2,
        compiler_params=params(), cost_estimate=cost(1e6, 3e6),
    )(a, b)


def join_kernel(a_ref, b_ref, out_ref):
    half = a_ref.shape[0]
    out_ref[:half] = a_ref[...]
    out_ref[half:] = b_ref[...]


def join(a, b, deps):
    vm = pl.BlockSpec(memory_space=pltpu.VMEM)
    return pl.pallas_call(
        with_deps(join_kernel, 2, len(deps)), name="join", in_specs=[vm] * 2 + [ANY] * len(deps), out_specs=vm,
        out_shape=shape_of((2 * a.shape[0], a.shape[1]), a.dtype), compiler_params=params(), cost_estimate=cost(1e6, 2e6),
    )(a, b, *deps)


def project_kernel(n1t_ref, *refs):
    w = jnp.concatenate([r[...] for r in in_order(refs[:8])], axis=0)
    out = dot(w, n1t_ref[...], TN).astype(BF)
    refs[8][...] = out.reshape(refs[8].shape)


def project(n1t, parts):
    width, rows = n1t.shape
    cols = 3 * width
    tile = 512
    return pl.pallas_call(
        project_kernel, grid=(cols // tile,), name="project",
        in_specs=[resident((width, rows))] + [pl.BlockSpec((p.shape[0], tile), lambda i: (0, i)) for p in parts],
        out_specs=pl.BlockSpec((tile // HEAD_DIM, HEAD_DIM, rows), lambda i: (i, 0, 0)),
        out_shape=shape_of((cols // HEAD_DIM, HEAD_DIM, rows), BF),
        compiler_params=params(), cost_estimate=cost(2 * rows * width * cols, 14e6),
    )(n1t, *parts)


def toeplitz(base_ref):
    row = lax.broadcasted_iota(jnp.int32, (T, T), 0)
    col = lax.broadcasted_iota(jnp.int32, (T, T), 1)
    count = base_ref.shape[1]
    rolled = [
        pltpu.roll(jnp.broadcast_to(base_ref[0, u:u + 1, :], (T, T)), 0, 1, stride=1, stride_axis=0)
        for u in range(count)
    ]
    return [jnp.where(col >= row, rolled[u], rolled[u + 1] if u + 1 < count else NEG) for u in range(count)]


def key_mask(len_ref, start):
    slot = start + lax.broadcasted_iota(jnp.int32, (T, 1), 0)
    return jnp.where(slot < len_ref[0], 0.0, NEG).astype(F32)


def attend_kernel(me_ref, len_ref, base_ref, q_ref, k_ref, v_ref, o_ref, lt_ref, g_ref):
    heads, tiles = base_ref.shape[:2]
    keys = [k_ref[h].T for h in range(heads)]
    for h in range(heads):
        for u, t in enumerate(toeplitz(base_ref.at[h:h + 1])):
            g_ref[h, u * T:(u + 1) * T, :] = t

    def scores(h, b):
        nk = (b + 1) * T
        q = q_ref[h, :, b * T:nk] * BF(HEAD_DIM ** -0.5)
        s = dot(keys[h][:nk], q) + g_ref[h, (tiles - 1 - b) * T:, :]
        if b == tiles - 1:
            s = jnp.concatenate([s[:b * T], s[b * T:] + key_mask(len_ref, b * T)], axis=0)
        return s, jnp.max(s, axis=0, keepdims=True)

    order = [(h, b) for b in range(tiles) for h in range(heads)]
    ahead = scores(*order[0])
    for n, (h, b) in enumerate(order):
        s, m = ahead
        if n + 1 < len(order):
            ahead = scores(*order[n + 1])
        sl = slice(b * T, (b + 1) * T)
        p = jnp.exp(s - m)
        total = jnp.sum(p, axis=0, keepdims=True)
        o = dot(v_ref[h, :, :(b + 1) * T], p.astype(BF))
        o_ref[h, :, sl] = (o * (1.0 / total)).astype(BF)
        lt_ref[h, :, sl] = m + jnp.log(total)


def head_place(h, me_ref):
    return jnp.bitwise_xor(h // 2, me_ref[0]) * 2 + h % 2


def attend(me, lengths, base, qkv):
    rows = qkv.shape[-1]
    tiles = rows // T
    pairs = HEADS // 2
    block = (2, HEAD_DIM, rows)
    at = lambda off: pl.BlockSpec(block, lambda h, m: (h + off, 0, 0))
    return pl.pallas_call(
        attend_kernel, name="attend",
        grid_spec=pltpu.PrefetchScalarGridSpec(
            num_scalar_prefetch=1, grid=(pairs,),
            in_specs=[SMEM, pl.BlockSpec((2, tiles, T), lambda h, m: (jnp.bitwise_xor(h, m[0]), 0, 0)), at(0), at(pairs), at(2 * pairs)],
            out_specs=[pl.BlockSpec(block, lambda h, m: (jnp.bitwise_xor(h, m[0]), 0, 0)),
                       pl.BlockSpec((2, 1, rows), lambda h, m: (h, 0, 0))],
            scratch_shapes=[pltpu.VMEM((2, rows, T), F32)]),
        out_shape=[shape_of((HEADS, HEAD_DIM, rows), BF), shape_of((HEADS, 1, rows), F32)],
        compiler_params=params(), cost_estimate=cost(30e9, 10e6),
    )(me, lengths, base, qkv, qkv, qkv)


def skew_sums(dg_ref, dist_ref):
    row = lax.broadcasted_iota(jnp.int32, (T, T), 0)
    col = lax.broadcasted_iota(jnp.int32, (T, T), 1)
    for u in range(dist_ref.shape[1]):
        z = jnp.where(col >= row, dg_ref[u * T:(u + 1) * T, :], dg_ref[(u - 1) * T:u * T, :] if u else 0.0)
        acc = z[0:8]
        for g in range(1, T // 8):
            acc = acc + pltpu.roll(z[8 * g:8 * g + 8], T - 8 * g, 1)
        tot = acc[0:1]
        for r in range(1, 8):
            tot = tot + pltpu.roll(acc[r:r + 1], T - r, 1)
        dist_ref[0, u:u + 1, :] = tot


def attend_back_kernel(me_ref, len_ref, base_ref, q_ref, k_ref, v_ref, o_ref, do_ref, lt_ref,
                       dq_ref, dk_ref, dv_ref, dist_ref, g_ref, dg_ref, dk_s, dv_s):
    tiles = base_ref.shape[1]
    scale = HEAD_DIM ** -0.5
    for u, t in enumerate(toeplitz(base_ref)):
        g_ref[u * T:(u + 1) * T, :] = t
    kt = k_ref[0]
    k = kt.T
    v = v_ref[0].T

    def scores(b):
        nk = (b + 1) * T
        sl = slice(b * T, nk)
        q = q_ref[0, :, sl] * BF(scale)
        do = do_ref[0, :, sl]
        inner = jnp.sum(do.astype(F32) * o_ref[0, :, sl].astype(F32), axis=0, keepdims=True)
        s = dot(k[:nk], q) + g_ref[(tiles - 1 - b) * T:, :]
        if b == tiles - 1:
            s = jnp.concatenate([s[:b * T], s[b * T:] + key_mask(len_ref, b * T)], axis=0)
        p = jnp.exp(s - lt_ref[0, :, sl])
        ds = p * (dot(v[:nk], do) - inner)
        return q, do, p.astype(BF), ds

    ahead = scores(tiles - 1)
    for b in range(tiles - 1, -1, -1):
        q, do, pb, ds = ahead
        if b:
            ahead = scores(b - 1)
        nk = (b + 1) * T
        low = (tiles - 1 - b) * T
        dsb = ds.astype(BF)
        dq_ref[0, :, b * T:nk] = (dot(kt[:, :nk], dsb) * scale).astype(BF)
        dvp = dot(do, pb, NT)
        dkp = dot(q, dsb, NT)
        if b == tiles - 1:
            dk_s[...] = dkp
            dv_s[...] = dvp
            dg_ref[...] = ds
        else:
            dk_s[:, :nk] += dkp
            dv_s[:, :nk] += dvp
            dg_ref[low:, :] += ds
    dk_ref[0] = dk_s[...].astype(BF)
    dv_ref[0] = dv_s[...].astype(BF)
    skew_sums(dg_ref, dist_ref)


def attend_back(me, lengths, base, qkv, o, do, lt, first, count, deps=()):
    rows = qkv.shape[-1]
    tiles = rows // T
    block = (1, HEAD_DIM, rows)
    at = lambda off: pl.BlockSpec(block, lambda h, m: (h + off + first, 0, 0))
    placed = pl.BlockSpec(block, lambda h, m: (head_place(h + first, m), 0, 0))
    out = pl.BlockSpec(block, lambda h, m: (h, 0, 0))
    return pl.pallas_call(
        with_deps(attend_back_kernel, 9, len(deps)), name="attend_back",
        grid_spec=pltpu.PrefetchScalarGridSpec(
            num_scalar_prefetch=1, grid=(count,),
            in_specs=[SMEM, pl.BlockSpec((1, tiles, T), lambda h, m: (head_place(h + first, m), 0, 0)), at(0), at(HEADS), at(2 * HEADS),
                      placed, placed, pl.BlockSpec((1, 1, rows), lambda h, m: (h + first, 0, 0))] + [ANY] * len(deps),
            out_specs=[out, out, out, pl.BlockSpec((1, tiles, T), lambda h, m: (h, 0, 0))],
            scratch_shapes=[pltpu.VMEM((rows, T), F32), pltpu.VMEM((rows, T), F32),
                            pltpu.VMEM((HEAD_DIM, rows), F32), pltpu.VMEM((HEAD_DIM, rows), F32)]),
        out_shape=[shape_of((count, HEAD_DIM, rows), BF)] * 3 + [shape_of((count, tiles, T), F32)],
        compiler_params=params(), cost_estimate=cost(2.4e9 * count, 1.2e6 * count),
    )(me, lengths, base, qkv, qkv, qkv, o, do, lt, *deps)


def middle_kernel(me_ref, at_ref, x_ref, gain_ref, shift_ref, *refs):
    parts, (mid_ref, n2_ref, n2t_ref, abs_s) = refs[:8], refs[8:]
    me = me_ref[0]
    w = jnp.concatenate([r[...] for r in in_order(parts)], axis=0)
    mid = x_ref[...].astype(F32) + dot(at_ref[...], w, TN)
    mid_ref[...] = mid
    hat, _ = normalise(mid)
    abs_s[...] = hat * gain_ref[...] + shift_ref[...]
    for r in range(8):
        sl = slice(r * 128, (r + 1) * 128)
        part = abs_s[:, pl.ds(block_of(me, r), 128)].astype(BF)
        n2_ref[:, sl] = part
        n2t_ref[sl, :] = part.T


def middle_of(me, at, x, gain, shift, parts, deps=()):
    rows, width = x.shape
    tile = pl.BlockSpec((T, width), lambda i: (i, 0))
    turned = pl.BlockSpec((width, T), lambda i: (0, i))
    return pl.pallas_call(
        with_deps(middle_kernel, 5 + len(parts), len(deps)), grid=(rows // T,), name="middle",
        in_specs=[SMEM, turned, tile, resident((1, width)), resident((1, width))] + [last_block(p, width) for p in parts]
        + [ANY] * len(deps),
        out_specs=[tile, tile, turned],
        out_shape=[shape_of((rows, width), F32), shape_of((rows, width), BF), shape_of((width, rows), BF)],
        scratch_shapes=[pltpu.VMEM((T, width), F32)],
        compiler_params=params(), cost_estimate=cost(2 * rows * width * width, 14e6),
    )(me, at, x, gain, shift, *parts, *deps)


def gelu_parts(x):
    a = jnp.abs(x)
    t = 1.0 / (1.0 + a * (0.3275911 * 0.7071067811865476))
    e = jnp.exp(x * x * -0.5)
    poly = t * (0.127414796 + t * (-0.142248368 + t * (0.7107068705 + t * (-0.7265760135 + t * 0.5307027145))))
    q = poly * e
    phi = jnp.where(x >= 0.0, 1.0 - q, q)
    return x * phi, phi + x * (e * 0.3989422804014327)


def feed_kernel(chunks, stacked, counts, me_ref, n2_h, n2t_h, og_h, w_h, *refs):
    carried, deps, n_out = counts
    carry, refs = refs[:carried], refs[carried + deps:]
    outs, refs = refs[:n_out], refs[n_out:]
    n2_v, n2t_v, og_v, w_v, g_v, hid_v, send_v, keep_v, sem_in, sem_out = refs
    me = me_ref[0]
    shard = [jnp.bitwise_xor(me, r) for r in range(8)]
    loads = [(n2_h, n2_v)]
    for part in (slice(0, 128), slice(128, 256)):
        loads += [(w_h.at[shard[r], chunks[0], part, :], w_v.at[r, 0, part, :]) for r in range(8)]
        if part.start == 0:
            loads.append((og_h, og_v))
    early = (9, 18)
    for k, c in enumerate(chunks[1:]):
        loads += [(w_h.at[shard[r], c], w_v.at[r, k + 1]) for r in range(8)]
    loads += list(zip(carry, (g_v,))) + [(n2t_h, n2t_v)]
    copies = [pltpu.make_async_copy(a, b, sem_in.at[i]) for i, (a, b) in enumerate(loads)]
    for x in copies:
        x.start()
    for x in copies[:early[0]]:
        x.wait()
    stores = []

    def store(a, b):
        stores.append(pltpu.make_async_copy(a, b, sem_out.at[len(stores)]))
        stores[-1].start()

    n2 = n2_v[...]
    steps = 2 * len(chunks)

    def products(t):
        k, u = t // 2, t % 2
        offs = [block_of(me, 4 * u + j) for j in range(4)]
        wi = jnp.concatenate([w_v[:, k, :128, pl.ds(o, 128)].reshape(1024, 128) for o in offs], axis=1)
        units = dot(n2, wi)
        if t == 0:
            for x in copies[early[0]:early[1]]:
                x.wait()
        wd = w_v[4 * u:4 * u + 4, k, 128:, :].reshape(512, 1024)
        return offs, wi, units, dot(og_v[...], wd, NT)

    ahead = products(0)
    og = og_v[...]
    for t in range(steps):
        k, u = t // 2, t % 2
        offs, wi, units, back = ahead
        if t + 1 < steps:
            ahead = products(t + 1)
        hid, slope = gelu_parts(units)
        hid = hid.astype(BF)
        pre = (back * slope).astype(BF)
        hid_v[:, t * 512:(t + 1) * 512] = hid
        store(hid_v.at[:, t * 512:(t + 1) * 512], outs[1].at[:, t * 512:(t + 1) * 512])
        if t == 0:
            for x in copies[early[1]:]:
                x.wait()
        if not carried and t == 0:
            g_v[...] = dot(pre, wi, NT)
        else:
            g_v[...] += dot(pre, wi, NT)
        if t == steps - 1:
            store(g_v, outs[0])
        dwi = dot(n2t_v[...], pre).astype(BF)
        for r in range(8):
            for j, o in enumerate(offs):
                (send_v if r % 2 else keep_v)[k, r // 2, :128, pl.ds(o, 128)] = dwi[r * 128:(r + 1) * 128, j * 128:(j + 1) * 128]
        if u == 1 and not stacked:
            for half, out in ((send_v, outs[2]), (keep_v, outs[3])):
                for b in range(4):
                    store(half.at[k, :, :128, b * 256:(b + 1) * 256], out.at[:, 8 * k + b])
        dwd = dot(hid, og, TN).astype(BF)
        for j in range(4):
            r = 4 * u + j
            (send_v if r % 2 else keep_v)[k, r // 2, 128:, :] = dwd[j * 128:(j + 1) * 128]
        if u == 1:
            if stacked:
                for r in range(8):
                    store((send_v if r % 2 else keep_v).at[k, r // 2], outs[2].at[shard[r], k])
            else:
                for half, out in ((send_v, outs[2]), (keep_v, outs[3])):
                    for b in range(4):
                        store(half.at[k, :, 128:, b * 256:(b + 1) * 256], out.at[:, 8 * k + 4 + b])
    for x in stores:
        x.wait()


def feed(chunks, stacked, me, n2, n2t, og, w, carry=(), deps=()):
    rows, width = n2.shape
    n = len(chunks)
    half = (n, 4, 256, 1024)
    grads = [(8, n, 256, 1024)] if stacked else [(4, 8 * n, 128, 256)] * 2
    counts = (len(carry), len(deps), 2 + len(grads))
    return pl.pallas_call(
        functools.partial(feed_kernel, chunks, stacked, counts), name="feed",
        in_specs=[SMEM] + [ANY] * (4 + len(carry) + len(deps)), out_specs=[ANY] * counts[2],
        out_shape=[shape_of((rows, width), F32), shape_of((rows, 1024 * n), BF)] + [shape_of(g, BF) for g in grads],
        scratch_shapes=[pltpu.VMEM((rows, width), BF), pltpu.VMEM((width, rows), BF), pltpu.VMEM((rows, width), BF),
                        pltpu.VMEM((8, n, 256, 1024), BF), pltpu.VMEM((rows, width), F32), pltpu.VMEM((rows, 1024 * n), BF),
                        pltpu.VMEM(half, BF), pltpu.VMEM(half, BF),
                        pltpu.SemaphoreType.DMA((20 + 8 * n,)), pltpu.SemaphoreType.DMA((20 * n + 1,))],
        compiler_params=params(), cost_estimate=cost(18e9 * n, 25e6),
    )(me, n2, n2t, og, w, *carry, *deps)


def output_kernel(me_ref, len_ref, mid_ref, *refs):
    hids, (w0_h, w1_h), (out_ref, w_v, sem) = refs[:-5], refs[-5:-3], refs[-3:]
    me = me_ref[0]
    i = pl.program_id(0)
    rows = mid_ref.shape[0]

    @pl.when(i == 0)
    def _():
        copies = []
        for k, h in enumerate((w0_h, w1_h)):
            for c in range(2):
                for r in range(8):
                    n = len(copies)
                    copies.append(pltpu.make_async_copy(
                        h.at[jnp.bitwise_xor(me, r), c, 128:, :], w_v.at[(2 * k + c) * 8 + r], sem.at[n]))
        for x in copies:
            x.start()
        for x in copies:
            x.wait()

    hid = jnp.concatenate([h[...] for h in hids], axis=1)
    total = mid_ref[...] + dot(hid, w_v[...].reshape(-1, w_v.shape[2]))
    slot = i * rows + lax.broadcasted_iota(jnp.int32, (rows, 1), 0)
    out_ref[...] = jnp.where(slot < len_ref[0], total, 0.0).astype(BF)


def output(me, lengths, mid, hids, w, deps=()):
    rows, width = mid.shape
    tile = pl.BlockSpec((T, width), lambda i: (i, 0))
    return pl.pallas_call(
        with_deps(output_kernel, 5 + len(hids), len(deps)), grid=(rows // T,), name="output",
        in_specs=[SMEM, SMEM, tile] + [pl.BlockSpec((T, h.shape[1]), lambda i: (i, 0)) for h in hids] + [ANY] * (2 + len(deps)),
        out_specs=tile, out_shape=shape_of((rows, width), BF),
        scratch_shapes=[pltpu.VMEM((32, 128, width), BF), pltpu.SemaphoreType.DMA((32,))],
        compiler_params=params(), cost_estimate=cost(9e9, 20e6),
    )(me, lengths, mid, *hids, *w, *deps)


def norm_back(hat, rstd, grad, gain):
    t = grad * gain
    return (t - jnp.mean(t, axis=-1, keepdims=True) - hat * jnp.mean(t * hat, axis=-1, keepdims=True)) * rstd


def middle_back_kernel(me_ref, mid_ref, g_ref, og_ref, at_ref, gain_ref, *refs):
    parts, (mg_ref, do_ref, send_ref, keep_ref, vec_ref, abs_s, acc_s) = refs[:8], refs[8:]
    me = me_ref[0]
    i = pl.program_id(0)
    for r in range(8):
        abs_s[:, pl.ds(block_of(me, r), 128)] = g_ref[:, r * 128:(r + 1) * 128]
    grad = abs_s[...]
    hat, rstd = normalise(mid_ref[...])
    sums = jnp.concatenate([jnp.sum(grad * hat, axis=0, keepdims=True), jnp.sum(grad, axis=0, keepdims=True)], axis=0)
    mg = og_ref[...].astype(F32) + norm_back(hat, rstd, grad, gain_ref[...])
    mg_ref[...] = mg
    branch = mg.astype(BF)
    w = jnp.concatenate([r[...] for r in in_order(parts)], axis=0)
    do_ref[...] = dot(w, branch, NT).astype(BF)
    dw = dot(at_ref[...], branch)

    @pl.when(i == 0)
    def _():
        vec_ref[...] = sums
        acc_s[...] = dw

    @pl.when(i > 0)
    def _():
        vec_ref[...] += sums
        acc_s[...] += dw

    @pl.when(i == pl.num_programs(0) - 1)
    def _():
        for r in range(8):
            for b in range(4):
                (send_ref if r % 2 else keep_ref)[r // 2, b] = acc_s[r * 128:(r + 1) * 128, b * 256:(b + 1) * 256].astype(BF)


def middle_back(me, mid, g, og, at, gain, parts, deps=()):
    rows, width = mid.shape
    tile = pl.BlockSpec((T, width), lambda i: (i, 0))
    turned = pl.BlockSpec((width, T), lambda i: (0, i))
    block = (4, 4, 128, 256)
    return pl.pallas_call(
        with_deps(middle_back_kernel, 6 + len(parts), len(deps)), grid=(rows // T,), name="middle_back",
        in_specs=[SMEM, tile, tile, tile, turned, resident((1, width))] + [last_block(p, width) for p in parts] + [ANY] * len(deps),
        out_specs=[tile, turned, resident(block), resident(block), resident((2, width))],
        out_shape=[shape_of((rows, width), F32), shape_of((width, rows), BF), shape_of(block, BF), shape_of(block, BF),
                   shape_of((2, width), F32)],
        scratch_shapes=[pltpu.VMEM((T, width), F32), pltpu.VMEM((width, width), F32)],
        compiler_params=params(), cost_estimate=cost(4 * rows * width * width, 24e6),
    )(me, mid, g, og, at, gain, *parts, *deps)


class Part:
    def __init__(self, array, start=0, count=None):
        self.array, self.start = array, start
        self.shape = ((array.shape[0] - start) if count is None else count,) + tuple(array.shape[1:])
        self.dtype = array.dtype

    def part(self, start, count):
        return Part(self.array, self.start + start, count)


def staged_kernel(steps, places, n_in, n_dep, n_out, where_ref, *refs):
    sources, refs = refs[:n_in], refs[n_in + n_dep:]
    dests, refs = refs[:n_out], refs[n_out:]
    n_kept = len(places)
    held, kept, sem_in, sem_out = refs[:n_in], refs[n_in:n_in + n_kept], refs[-2], refs[-1]
    loads = []
    for ins, _, _ in steps:
        for p in ins:
            k = len(loads)
            loads.append(pltpu.make_async_copy(sources[k].at[p.start:p.start + p.shape[0]], held[k], sem_in.at[k]))
    for c in loads:
        c.start()
    stores = []
    a = b = 0
    for ins, outs, fn in steps:
        for c in loads[a:a + len(ins)]:
            c.wait()
        fn(where_ref, held[a:a + len(ins)], kept[b:b + len(outs)])
        for k in range(b, b + len(outs)):
            n, start = places[k]
            stores.append(pltpu.make_async_copy(kept[k], dests[n].at[start:start + kept[k].shape[0]], sem_out.at[k]))
            stores[-1].start()
        a += len(ins)
        b += len(outs)
    for c in stores:
        c.wait()


def staged(where, steps, deps=()):
    steps = [([v if isinstance(v, Part) else Part(v) for v in ins], outs, fn) for ins, outs, fn in steps]
    parts = [v for ins, _, _ in steps for v in ins]
    flat = [o for _, outs, _ in steps for o in outs]
    arrays, places, by_way = [], [], {}
    for way, shape, kind in flat:
        if way is None:
            places.append((len(arrays), 0))
            arrays.append(shape_of(shape, kind))
            continue
        key = (way,) + tuple(shape[1:]) + (kind,)
        if key not in by_way:
            by_way[key] = len(arrays)
            arrays.append(shape_of((0,) + tuple(shape[1:]), kind))
        n = by_way[key]
        places.append((n, arrays[n].shape[0]))
        arrays[n] = shape_of((arrays[n].shape[0] + shape[0],) + tuple(shape[1:]), kind)
    out = pl.pallas_call(
        functools.partial(staged_kernel, steps, places, len(parts), len(deps), len(arrays)), name="staged",
        in_specs=[SMEM] + [ANY] * (len(parts) + len(deps)), out_specs=[ANY] * len(arrays), out_shape=arrays,
        scratch_shapes=[pltpu.VMEM(v.shape, v.dtype) for v in parts] + [pltpu.VMEM(o[1], o[2]) for o in flat]
        + [pltpu.SemaphoreType.DMA((len(parts),)), pltpu.SemaphoreType.DMA((len(flat),))],
        compiler_params=params(), cost_estimate=cost(3e9, 10e6),
    )(where, *(p.array for p in parts), *deps)
    sent = list(out)
    for key, n in by_way.items():
        sent[n] = send(out[n], key[0])
    flat = [[Part(v, start, o[1][0]) for v in sent[n]] if o[0] == "turns" else Part(sent[n], start, o[1][0])
            for (n, start), o in zip(places, flat)]
    result = []
    for _, o, _ in steps:
        result.append(flat[:len(o)])
        flat = flat[len(o):]
    return result, tuple(out)


def send(v, way):
    if way in ("core", "x", "y", "both"):
        return flip(v, {"core": 1, "x": 2, "y": 4, "both": 6}[way])
    if way == "turns":
        return copy_turns(v, 4)
    k = {"pair": 1, "far": 2}[way]
    return lax.ppermute(v, "rep", [(i, i ^ k) for i in range(4)])


def plus(*refs):
    total = refs[0].astype(F32)
    for r in refs[1:]:
        total = total + r.astype(F32)
    return total


def project_back(n1t, three, way):
    block = (12, 128, 256)

    def fn(_, ins, outs):
        n1 = ins[0][...]
        for j in range(3):
            dw = dot(n1, ins[1 + j][...], NT).astype(BF)
            for r in range(8):
                outs[r % 2 == 0][r // 2 * 3 + j] = dw[r * 128:(r + 1) * 128]

    return [n1t, *three], [(way, block, BF), (None, block, BF)], fn


def put(out, v):
    nb, rows = v.shape[0], out.shape[1]
    for k in range(out.shape[0] // nb):
        out[k * nb:(k + 1) * nb] = v[:, k * rows:(k + 1) * rows]


def whole(v):
    nb = v.shape[0] * v.shape[1] // 128
    return jnp.concatenate([v[k * nb:(k + 1) * nb] for k in range(128 // v.shape[1])], axis=1)


class Piece:
    def __init__(self, nb, keep, got, straight, copies):
        self.nb, self.keep, self.got = nb, keep, got
        self.plan = ["straight", "straight_sum"] if straight else ["sums", "second", "shard"]
        self.plan += {"halves": ["quarter", "quarter_back", "half_back"], "pairs": ["far"], "turns": []}[copies]
        self.copies = copies

    def step(self):
        return getattr(self, self.plan.pop(0))()

    def take(self, result):
        self.got = result

    def sums(self):
        nb = self.nb

        def fn(_, ins, outs):
            k, g = ins
            for out, half, pair in zip(outs, (0, 1, 0, 1), ((1, 3), (2, 3), (0, 2), (0, 1))):
                rows = slice(half * 64, half * 64 + 64)
                for n, j in enumerate(pair):
                    at = slice(j * nb, (j + 1) * nb)
                    out[n * nb:(n + 1) * nb] = plus(k[at, rows, :], g[at, rows, :]).astype(BF)

        out = (2 * nb, 64, 256)
        return [self.keep, self.got], [("x", out, BF), ("y", out, BF), (None, out, BF), (None, out, BF)], fn

    def second(self):
        nb = self.nb
        gx, gy, a, b = self.got
        self.rest = (a.part(0, nb), gx.part(0, nb), b.part(0, nb), gy.part(0, nb))

        def fn(_, ins, outs):
            outs[0][...] = plus(ins[0][...], ins[1][...]).astype(BF)
            outs[1][...] = plus(ins[2][...], ins[3][...]).astype(BF)

        out = (nb, 64, 256)
        ins = [v.part(nb, nb) for v in (a, gx, b, gy)]
        return ins, [("y", out, BF), ("x", out, BF)], fn

    def shard(self):
        a, gx, b, gy = self.rest

        def fn(where, ins, outs):
            a = plus(ins[0][...], ins[1][...], ins[2][...]).astype(BF)
            b = plus(ins[3][...], ins[4][...], ins[5][...]).astype(BF)
            self.first_copies(where, outs, a, b)

        return [a, gx, self.got[0], b, gy, self.got[1]], self.first_outs(), fn

    def straight(self):
        nb = self.nb

        def fn(_, ins, outs):
            for out, j in zip(outs, (1, 2, 3, 0)):
                at = slice(j * nb, (j + 1) * nb)
                put(out, plus(ins[0][at], ins[1][at]).astype(BF))

        out = (2 * nb, 64, 256)
        return [self.keep, self.got], [(way, out, BF) for way in ("x", "y", "both", None)], fn

    def straight_sum(self):
        nb = self.nb

        def fn(where, ins, outs):
            v = plus(*(r[...] for r in ins)).astype(BF)
            self.first_copies(where, outs, v[:nb], v[nb:])

        return list(self.got), self.first_outs(), fn

    def first_outs(self):
        nb = self.nb
        out = ((nb if self.copies == "halves" else 2 * nb), 64, 256)
        return [("turns" if self.copies == "turns" else "pair", out, BF), (None, out, BF)]

    def first_copies(self, where, outs, a, b):
        nb = self.nb
        if self.copies == "halves":
            odd = where[1] == 1
            outs[0][...] = jnp.where(odd, a, b)
            outs[1][...] = jnp.where(odd, b, a)
        else:
            for out in outs:
                out[:nb] = a
                out[nb:] = b

    def far(self):
        def fn(_, ins, outs):
            v = whole(plus(ins[0][...], ins[1][...]).astype(BF))
            for out in outs:
                put(out, v)

        out = (4 * self.nb, 32, 256)
        return list(self.got), [("far", out, BF), (None, out, BF)], fn

    def quarter(self):
        def fn(where, ins, outs):
            a = plus(ins[0][:, :32], ins[1][:, :32]).astype(BF)
            b = plus(ins[0][:, 32:], ins[1][:, 32:]).astype(BF)
            high = where[2] == 1
            outs[0][...] = jnp.where(high, a, b)
            outs[1][...] = jnp.where(high, b, a)

        out = (self.nb, 32, 256)
        return list(self.got), [("far", out, BF), (None, out, BF)], fn

    def quarter_back(self):
        def fn(_, ins, outs):
            v = plus(ins[0][...], ins[1][...]).astype(BF)
            outs[0][...] = v
            outs[1][...] = v

        out = (self.nb, 32, 256)
        return list(self.got), [("far", out, BF), (None, out, BF)], fn

    def half_back(self):
        def fn(where, ins, outs):
            high = where[2] == 1
            got, mine = ins[0][...], ins[1][...]
            for out in outs:
                out[:, :32] = jnp.where(high, got, mine)
                out[:, 32:] = jnp.where(high, mine, got)

        out = (self.nb, 64, 256)
        return list(self.got), [("pair", out, BF), (None, out, BF)], fn

    def final(self):
        nb, copies = self.nb, self.copies
        ins = (list(self.got[0]) + [self.got[1]]) if copies == "turns" else list(self.got)

        def value(where, ins, b):
            if copies != "halves":
                rows = ins[0].shape[1]
                return jnp.concatenate([plus(*(r[k * nb + b] for r in ins)) for k in range(128 // rows)]).astype(BF).astype(F32)
            odd = where[1] == 1
            got, mine = ins[0][b].astype(F32), ins[1][b].astype(F32)
            return jnp.concatenate([jnp.where(odd, got, mine), jnp.where(odd, mine, got)])

        return ins, value


def finish_kernel(groups, me_ref, x_ref, mg_ref, gain_ref, *refs):
    parts, refs = refs[:8], refs[8:]
    grads, (ig_ref, vec_ref, abs_s) = refs[:3 * groups], refs[3 * groups:]
    me = me_ref[0]
    i = pl.program_id(0)
    rows, width = x_ref.shape
    w = jnp.concatenate([r[...] for r in in_order(parts)], axis=0)
    pg = jnp.concatenate([grads[3 * g + j][...] for j in range(3) for g in range(groups)], axis=0)
    total = dot(pg, w, TT)
    for r in range(8):
        abs_s[:, pl.ds(block_of(me, r), 128)] = total[:, r * 128:(r + 1) * 128]
    grad = abs_s[...]
    hat, rstd = normalise(x_ref[...].astype(F32))
    sums = jnp.concatenate([jnp.sum(grad * hat, axis=0, keepdims=True), jnp.sum(grad, axis=0, keepdims=True)], axis=0)
    ig_ref[...] = mg_ref[...] + norm_back(hat, rstd, grad, gain_ref[...])

    @pl.when(i == 0)
    def _():
        vec_ref[...] = sums

    @pl.when(i > 0)
    def _():
        vec_ref[...] += sums


def finish(me, x, mg, gain, parts, grads, deps=()):
    rows, width = x.shape
    tile = pl.BlockSpec((T, width), lambda i: (i, 0))
    return pl.pallas_call(
        with_deps(functools.partial(finish_kernel, len(grads) // 3), 4 + len(parts) + len(grads), len(deps)),
        grid=(rows // T,), name="finish",
        in_specs=[SMEM, tile, tile, resident((1, width))] + [resident((p.shape[0], 3 * width)) for p in parts]
        + [pl.BlockSpec((g.shape[0], T), lambda i: (0, i)) for g in grads] + [ANY] * len(deps),
        out_specs=[tile, resident((2, width))],
        out_shape=[shape_of((rows, width), F32), shape_of((2, width), F32)],
        scratch_shapes=[pltpu.VMEM((T, width), F32)],
        compiler_params=params(), cost_estimate=cost(6 * rows * width * width, 34e6),
    )(me, x, mg, gain, *parts, *grads, *deps)


def flip(v, k):
    return lax.ppermute(v, "fsdp", [(i, i ^ k) for i in range(GROUPS)])


def xor_rows(v, me):
    for k in (1, 2, 4):
        turned = v.reshape((8 // (2 * k), 2, k) + v.shape[1:])[:, ::-1].reshape(v.shape)
        v = jnp.where((me & k) != 0, turned, v)
    return v


def split_full(full):
    m = full.shape[0] // 8
    return [full[r * m:(r + 1) * m] for r in PLACES]


def vector_sums(vec_one, vec_two, dists, buckets):
    def fn(where, ins, outs):
        by = jnp.concatenate([jnp.concatenate([d[:, u, :] for u in range(d.shape[1] - 1, -1, -1)], axis=1) for d in ins[2:-1]])
        onehot = (ins[-1][...] == lax.broadcasted_iota(jnp.int32, (BUCKETS, by.shape[1]), 0)).astype(F32)
        table = lax.dot_general(by, onehot, NT, precision=lax.Precision.HIGHEST, preferred_element_type=F32)
        table_s, row_s = outs[2:]
        table_s[...] = jnp.concatenate([jnp.concatenate([table[2 * r:2 * r + 1], table[2 * r + 1:2 * r + 2]], axis=1) for r in range(8)])
        row_s[...] = jnp.zeros_like(row_s)
        for out in outs[:2]:
            out[...] = jnp.zeros_like(out)
        for r in range(8):
            at = pl.ds(block_of(where[0], r), 128)
            for k in range(4):
                row_s[k // 2:k // 2 + 1, k % 2 * 128:(k % 2 + 1) * 128] = ins[k // 2][k % 2:k % 2 + 1, at]
            row_s[2:3, :64] = table_s[pl.ds(jnp.bitwise_xor(where[0], r), 1), :]
            outs[1 - r % 2][r // 2, :16, :] = row_s[...].astype(BF)

    out = (4, 128, 256)
    return [vec_one, vec_two, *dists, buckets], [
        ("core", out, BF), (None, out, BF), (None, (8, 64), F32), (None, (16, 256), F32)], fn


def vector_result(piece):
    mine, value = piece.final()

    def fn(where, ins, outs):
        v = value(where, ins, 0)
        for k in range(4):
            outs[k][...] = v[k // 2:k // 2 + 1, k % 2 * 128:(k % 2 + 1) * 128]
        outs[4][...] = v[2:3, :64]

    return mine, [(None, (1, 128), F32)] * 4 + [(None, (1, 64), F32)], fn


def feed_result(one, pieces):
    finals = [p.final() for p in pieces]

    def fn(where, ins, outs):
        for c in range(2):
            base = c * 256
            for b in range(8):
                col = (b * CHUNKS + c) * 128
                outs[0][:, col:col + 128] = ins[0][base:base + 128, b * 128:(b + 1) * 128].astype(F32)
            outs[1][c * 128:(c + 1) * 128, :] = ins[0][base + 128:base + 256, :].astype(F32)
        at = 1
        for c, (mine, value) in zip((2, 3), finals):
            refs = ins[at:at + len(mine)]
            at += len(mine)
            for b in range(4):
                v = value(where, refs, b)
                for k in range(2):
                    col = ((2 * b + k) * CHUNKS + c) * 128
                    outs[0][:, col:col + 128] = v[:, k * 128:(k + 1) * 128]
                outs[1][c * 128:(c + 1) * 128, b * 256:(b + 1) * 256] = value(where, refs, 4 + b)

    return [one] + [v for mine, _ in finals for v in mine], [(None, (128, 4096), F32), (None, (512, 1024), F32)], fn


def project_result(out_piece, pieces):
    finals = [p.final() for p in [out_piece] + pieces]

    def fn(where, ins, outs):
        at = 0
        for g, (mine, value) in enumerate(finals):
            refs = ins[at:at + len(mine)]
            at += len(mine)
            for b in range(3 if g else 4):
                col = (b * HEAD_GROUPS + g - 1) * 256 if g else b * 256
                outs[0 if g else 1][:, col:col + 256] = value(where, refs, b)

    return [v for mine, _ in finals for v in mine], [(None, (128, 3072), F32), (None, (128, 1024), F32)], fn


def copy_turns(v, count):
    return [lax.ppermute(v, "rep", [(i, (i + k) % count) for i in range(count)]) for k in range(1, count)]


def per_device(n_fsdp, n_rep, inputs, lengths, bucket_table, ln1_gain, ln1_shift, w_qkv, rel_bias, w_out, ln2_gain, ln2_shift,
               w_in, w_down, cotangent):
    near = n_fsdp == GROUPS and n_rep == 4
    _, slots, width = inputs.shape
    hidden = w_in.shape[1]
    me = lax.axis_index("fsdp").astype(jnp.int32) if near else jnp.int32(0)
    me1 = me.reshape(1)
    x = inputs.reshape(slots, width)
    cot = cotangent.reshape(slots, width)
    full = lambda w: lax.all_gather(w, "fsdp", axis=0, tiled=True)

    if near:
        piece, own = lead(w_qkv, w_out, ln1_gain, ln1_shift, ln2_gain, ln2_shift, rel_bias)
        small = jnp.concatenate([own] + [flip(own, k) for k in (2, 4, 6)])
        small = jnp.stack([small, flip(small, 1)], axis=1).reshape(8, -1)
        r2, r4 = flip(piece, 2), flip(piece, 4)
        h2, h4 = halves(r2, r4)
        r6a, r6b = flip(h2, 4), flip(h4, 2)
        n1t, og, vecs, base = prepare(me1, lengths, x, cot, bucket_table[None], small, (h2, h4))
        ffn_w = [full(v.reshape(512, 1024)).reshape(8, 2, 256, 1024) for v in pack(w_in, w_down, (h2, h4))]
        parts = [piece, r2, r4, join(r6a, r6b, (n1t,))]
        parts = parts + [flip(v, 1) for v in parts]
    else:
        n = ln1_gain.shape[0]
        small = full(jnp.concatenate([ln1_gain, ln1_shift, ln2_gain, ln2_shift, rel_bias])[None])
        small = jnp.concatenate([small[:, i * n:(i + 1) * n].reshape(8, 128) for i in range(4)] + [small[:, 4 * n:].reshape(8, 64)], axis=1)
        n1t, og, vecs, base = prepare(me1, lengths, x, cot, bucket_table[None], small)
        parts = split_full(jnp.concatenate([full(w_qkv), full(w_out)], axis=1))
        wi_c = full(w_in).reshape(8, width // 8, 8, CHUNKS, 128)
        wd_c = full(w_down).reshape(8, CHUNKS, 128, width)
        chunk = [jnp.concatenate([wi_c[:, :, :, c].reshape(8, width // 8, 1024), wd_c[:, c]], axis=1) for c in range(CHUNKS)]
        ffn_w = [jnp.stack(chunk[2 * h:2 * h + 2], axis=1) for h in range(2)]
    n = ln1_gain.shape[0]
    gain_one, shift_one, gain_two, shift_two = (vecs[i:i + 1] for i in range(4))
    qkv = project(n1t, parts)
    o, lt = attend(me1, lengths, base, qkv)
    at = o.reshape(width, slots)
    mid, n2, n2t = middle_of(me1, at, x, gain_two, shift_two, parts)
    grads, dists = [], []
    rep = lax.axis_index("rep").astype(jnp.int32)
    where = jnp.stack([me, rep % 2, rep // 2])
    per = HEADS // HEAD_GROUPS
    last = ffn_w[1]

    def back(k, deps=()):
        *three, dist = attend_back(me1, lengths, base, qkv, o, do, lt, k * per, per, deps)
        three = [v.reshape(per * HEAD_DIM, slots) for v in three]
        grads.extend(three)
        dists.append(dist)
        return three

    def slot(pieces, before=(), after=(), deps=()):
        result, made = staged(where, list(before) + [p.step() for p in pieces] + list(after), deps)
        for p, r in zip(pieces, result[len(before):]):
            p.take(r)
        return result[:len(before)] + result[len(before) + len(pieces):], made

    g, hid1, one = feed((0, 1), True, me1, n2, n2t, og, ffn_w[0])
    if near:
        one = lax.psum_scatter(one.reshape(8 * 512, 1024), "fsdp", scatter_dimension=0, tiled=True)
        blocks = lambda v: v.reshape((-1,) + v.shape[2:])
        start = lambda nb, away, keep, *plan: Piece(nb, Part(blocks(keep)), Part(flip(blocks(away), 1)), *plan)
        g, hid2, away, keep = feed((0,), False, me1, n2, n2t, og, last, (g,))
        f2 = start(8, away, keep, False, "halves")
        g, hid3, away, keep = feed((1,), False, me1, n2, n2t, og, last, (g,))
        f3 = start(8, away, keep, False, "halves")
        _, made = slot([f2], deps=(g,))
        mg, do, away, keep, vec_two = middle_back(me1, mid, g, og, at, gain_two, parts, made)
        do = do.reshape(HEADS, HEAD_DIM, slots)
        wo = start(4, away, keep, False, "pairs")
        _, made = slot([f3], deps=(mg,))
        three = back(0, made)
        ((got, keep),), made = slot([f2, f3], [project_back(n1t, three, "core")], deps=(one,))
        one = lax.psum(one, "rep")
        q0 = Piece(3, keep, got, False, "pairs")
        three = back(1, made)
        ((got, keep),), made = slot([f2, f3, wo, q0], [project_back(n1t, three, "core")])
        q1 = Piece(3, keep, got, False, "pairs")
        three = back(2, made)
        ((got, keep),), made = slot([f2, f3, wo, q0, q1], [project_back(n1t, three, "core")])
        q2 = Piece(3, keep, got, True, "pairs")
        three = back(3, made)
        ((got, keep),), made = slot([f2, f3, wo, q0, q1, q2], [project_back(n1t, three, "core")])
        q3 = Piece(3, keep, got, True, "pairs")
        input_grad, vec_one = finish(me1, x, mg, gain_one, parts, grads, made)
        ((got, keep, *_),), made = slot([], [vector_sums(vec_one, vec_two, dists, bucket_table[None])])
        vec = Piece(1, keep, got, True, "pairs")
        came = lambda *pieces: tuple(p.got[0].array for p in pieces)
        _, made = slot([q3, q2, f2, f3, wo, q0, q1, vec], deps=(one,))
        outputs = output(me1, lengths, mid, [hid1, hid2, hid3], ffn_w, made)
        ((in_grad, down_grad),), made = slot([q3, vec, q2, q1], [], [feed_result(one, [f2, f3])], deps=(outputs,) + came(wo, q0))
        _, made = slot([q3, vec], deps=came(q2, q1))
        ((qkv_grad, out_g), tiny), _ = slot([], [project_result(wo, [q0, q1, q2, q3]), vector_result(vec)])
        in_grad, down_grad, qkv_grad, out_g = (v.array for v in (in_grad, down_grad, qkv_grad, out_g))
        tiny = [v.array[0] for v in tiny]
    else:
        g, hid2, two = feed((0, 1), True, me1, n2, n2t, og, last, (g,))
        mg, do, away, keep, vec_two = middle_back(me1, mid, g, og, at, gain_two, parts)
        do = do.reshape(HEADS, HEAD_DIM, slots)
        pieces = [staged(where, [project_back(n1t, back(k), None)])[0][0] for k in range(HEAD_GROUPS)]
        input_grad, vec_one = finish(me1, x, mg, gain_one, parts, grads)
        outputs = output(me1, lengths, mid, [hid1, hid2], ffn_w)
        onehot = (bucket_table[:, None] == lax.iota(jnp.int32, BUCKETS)[None, :]).astype(F32)
        distance_total = jnp.concatenate(dists)[:, ::-1].reshape(HEADS, slots)
        table_grad = jnp.dot(distance_total, onehot, precision=lax.Precision.HIGHEST, preferred_element_type=F32)
        vec = jnp.concatenate([v.reshape(n_fsdp, -1) for v in (vec_one[0], vec_one[1], vec_two[0], vec_two[1], table_grad)], axis=1)
        reduced = lambda v: lax.psum(lax.psum_scatter(v, "fsdp", scatter_dimension=0, tiled=True), "rep")
        tiny = reduced(vec)[0]
        tiny = [tiny[k * n:(k + 1) * n] for k in range(4)] + [tiny[4 * n:]]
        stack = jnp.concatenate([one, two], axis=1)
        in_grad = reduced(stack[:, :, :128].reshape(8, CHUNKS, 128, 8, 128).transpose(0, 2, 3, 1, 4).reshape(width, hidden))
        down_grad = reduced(stack[:, :, 128:].reshape(hidden, width))
        whole = lambda away, keep: jnp.stack([keep, away], axis=1).reshape((8,) + keep.shape[1:]).swapaxes(1, 2)
        out_g = reduced(whole(away, keep).reshape(width, width))
        columns = [whole(*(v.array.reshape(4, 3, 128, 256) for v in p)) for p in pieces]
        qkv_grad = reduced(jnp.stack(columns, axis=3).reshape(width, 3 * width))
    return (outputs.reshape(inputs.shape), input_grad.reshape(inputs.shape), tiny[0], tiny[1], qkv_grad.astype(F32),
            tiny[4], out_g.astype(F32), tiny[2], tiny[3], in_grad.astype(F32), down_grad.astype(F32))


def solution(mesh):
    rows = P(("rep", "fsdp"), None, None)
    vec = P("fsdp")
    mat = P("fsdp", None)
    return jax.shard_map(
        functools.partial(per_device, mesh.shape["fsdp"], mesh.shape["rep"]),
        mesh=mesh,
        in_specs=(rows, P(("rep", "fsdp")), P(), vec, vec, mat, vec, mat, vec, vec, mat, mat, rows),
        out_specs=(rows, rows, vec, vec, mat, vec, mat, vec, vec, mat, mat),
        check_vma=False,
    )
```

```python
import functools

import jax
import jax.numpy as jnp
from jax import lax
from jax.experimental import pallas as pl
from jax.experimental.pallas import tpu as pltpu
from jax.sharding import PartitionSpec as P

HEADS = 16
HEAD_DIM = 64
BUCKETS = 32
T = 256
NEG = -1e30
F32 = jnp.float32
BF = jnp.bfloat16
GROUPS = 8
CHUNKS = 4
HEAD_GROUPS = 4
NN = (((1,), (0,)), ((), ()))
NT = (((1,), (1,)), ((), ()))
TN = (((0,), (0,)), ((), ()))
TT = (((0,), (1,)), ((), ()))
ANY = pl.BlockSpec(memory_space=pl.ANY)
SMEM = pl.BlockSpec(memory_space=pltpu.SMEM)


def dot(a, b, form=NN):
    return lax.dot_general(a, b, form, preferred_element_type=F32)


def params(mib=60):
    return pltpu.CompilerParams(vmem_limit_bytes=mib << 20)


def cost(flops, moved, exps=0):
    return pl.CostEstimate(flops=int(flops), bytes_accessed=int(moved), transcendentals=int(exps))


def resident(shape):
    return pl.BlockSpec(shape, lambda i, *_: (0,) * len(shape))


def shape_of(shape, kind):
    return jax.ShapeDtypeStruct(shape, kind)


def last_block(part, width):
    at = part.shape[1] // width - 1
    return pl.BlockSpec((part.shape[0], width), lambda i: (0, at))


def block_of(me, r):
    return pl.multiple_of(jnp.bitwise_xor(me, r) * 128, 128)


PLACES = (0, 2, 4, 6, 1, 3, 5, 7)


def in_order(parts):
    return [parts[PLACES.index(r)] for r in range(8)]


def normalise(v):
    centred = v - jnp.mean(v, axis=-1, keepdims=True)
    rstd = lax.rsqrt(jnp.mean(centred * centred, axis=-1, keepdims=True) + 1e-5)
    return centred * rstd, rstd


def with_deps(kernel, inputs, count):
    def body(*refs):
        return kernel(*refs[:inputs], *refs[inputs + count:])
    return body


def prepare_kernel(me_ref, len_ref, x_ref, cot_ref, bucket_ref, *refs):
    small_ref, n1t_ref, og_ref, vec_ref, base_ref, abs_s = refs
    me = me_ref[0]
    rows = x_ref.shape[0]

    @pl.when(pl.program_id(0) == 0)
    def _():
        small = small_ref[...].astype(F32)
        for r in range(8):
            for k in range(4):
                vec_ref[k:k + 1, pl.ds(block_of(me, r), 128)] = small[r:r + 1, k * 128:(k + 1) * 128]
        table = jnp.concatenate([
            small[h // 2:h // 2 + 1, 512 + h % 2 * BUCKETS:512 + (h % 2 + 1) * BUCKETS] for h in range(HEADS)]).astype(BF)
        slots = bucket_ref.shape[1]
        onehot = (bucket_ref[...] == lax.broadcasted_iota(jnp.int32, (BUCKETS, slots), 0)).astype(BF)
        by = dot(table, onehot)
        for u in range(slots // T):
            base_ref[:, u, :] = by[:, slots - (u + 1) * T:slots - u * T]

    hat, _ = normalise(x_ref[...].astype(F32))
    abs_s[...] = hat * vec_ref[0:1] + vec_ref[1:2]
    for r in range(8):
        n1t_ref[r * 128:(r + 1) * 128, :] = abs_s[:, pl.ds(block_of(me, r), 128)].astype(BF).T
    slot = pl.program_id(0) * rows + lax.broadcasted_iota(jnp.int32, (rows, 1), 0)
    og_ref[...] = jnp.where(slot < len_ref[0], cot_ref[...], jnp.zeros_like(cot_ref))


def prepare(me, lengths, x, cot, buckets, small, deps=()):
    rows, width = x.shape
    tile = pl.BlockSpec((T, width), lambda i: (i, 0))
    return pl.pallas_call(
        with_deps(prepare_kernel, 6, len(deps)), grid=(rows // T,), name="prepare",
        in_specs=[SMEM, SMEM, tile, tile, resident(buckets.shape), resident(small.shape)] + [ANY] * len(deps),
        out_specs=[pl.BlockSpec((width, T), lambda i: (0, i)), tile, resident((4, width)), resident((HEADS, rows // T, T))],
        out_shape=[shape_of((width, rows), BF), shape_of((rows, width), BF), shape_of((4, width), F32),
                   shape_of((HEADS, rows // T, T), F32)],
        scratch_shapes=[pltpu.VMEM((T, width), F32)],
        compiler_params=params(), cost_estimate=cost(1e9, 8e6),
    )(me, lengths, x, cot, buckets, small, *deps)


def pack_kernel(wi_ref, wd_ref, *refs):
    for c, out in enumerate(refs):
        for k in range(2):
            for b in range(8):
                col = (b * CHUNKS + 2 * c + k) * 128
                out[k, :128, b * 128:(b + 1) * 128] = wi_ref[:, col:col + 128]
            out[k, 128:, :] = wd_ref[(2 * c + k) * 128:(2 * c + k + 1) * 128, :]


def pack(w_in, w_down, deps):
    vm = pl.BlockSpec(memory_space=pltpu.VMEM)
    return pl.pallas_call(
        with_deps(pack_kernel, 2, len(deps)), name="pack", in_specs=[vm] * 2 + [ANY] * len(deps), out_specs=[vm] * 2,
        out_shape=[shape_of((2, 256, 1024), BF)] * 2, compiler_params=params(), cost_estimate=cost(1e6, 4e6),
    )(w_in, w_down, *deps)


def lead_kernel(qkv_ref, out_ref, a_ref, b_ref, c_ref, d_ref, e_ref, piece_ref, small_ref):
    cols = qkv_ref.shape[1]
    piece_ref[:, :cols] = qkv_ref[...]
    piece_ref[:, cols:] = out_ref[...]
    at = 0
    for ref in (a_ref, b_ref, c_ref, d_ref, e_ref):
        small_ref[:, at:at + ref.shape[1]] = ref[...]
        at += ref.shape[1]


def lead(w_qkv, w_out, *small):
    vm = pl.BlockSpec(memory_space=pltpu.VMEM)
    rows, cols = w_qkv.shape[0], w_qkv.shape[1] + w_out.shape[1]
    small = [v[None] for v in small]
    return pl.pallas_call(
        lead_kernel, name="lead", in_specs=[vm] * 7, out_specs=[vm] * 2,
        out_shape=[shape_of((rows, cols), BF), shape_of((1, sum(v.shape[1] for v in small)), BF)],
        compiler_params=params(), cost_estimate=cost(1e6, 2e6),
    )(w_qkv, w_out, *small)


def halves_kernel(a_ref, b_ref, a_out, b_out):
    half = a_out.shape[0]
    a_out[...] = a_ref[:half]
    b_out[...] = b_ref[half:]


def halves(a, b):
    vm = pl.BlockSpec(memory_space=pltpu.VMEM)
    out = shape_of((a.shape[0] // 2, a.shape[1]), a.dtype)
    return pl.pallas_call(
        halves_kernel, name="halves", in_specs=[vm] * 2, out_specs=[vm] * 2, out_shape=[out] * 2,
        compiler_params=params(), cost_estimate=cost(1e6, 3e6),
    )(a, b)


def join_kernel(a_ref, b_ref, out_ref):
    half = a_ref.shape[0]
    out_ref[:half] = a_ref[...]
    out_ref[half:] = b_ref[...]


def join(a, b, deps):
    vm = pl.BlockSpec(memory_space=pltpu.VMEM)
    return pl.pallas_call(
        with_deps(join_kernel, 2, len(deps)), name="join", in_specs=[vm] * 2 + [ANY] * len(deps), out_specs=vm,
        out_shape=shape_of((2 * a.shape[0], a.shape[1]), a.dtype), compiler_params=params(), cost_estimate=cost(1e6, 2e6),
    )(a, b, *deps)


def project_kernel(n1t_ref, *refs):
    w = jnp.concatenate([r[...] for r in in_order(refs[:8])], axis=0)
    out = dot(w, n1t_ref[...], TN).astype(BF)
    refs[8][...] = out.reshape(refs[8].shape)


def project(n1t, parts):
    width, rows = n1t.shape
    cols = 3 * width
    tile = 1024
    return pl.pallas_call(
        project_kernel, grid=(cols // tile,), name="project",
        in_specs=[resident((width, rows))] + [pl.BlockSpec((p.shape[0], tile), lambda i: (0, i)) for p in parts],
        out_specs=pl.BlockSpec((tile // HEAD_DIM, HEAD_DIM, rows), lambda i: (i, 0, 0)),
        out_shape=shape_of((cols // HEAD_DIM, HEAD_DIM, rows), BF),
        compiler_params=params(), cost_estimate=cost(2 * rows * width * cols, 14e6),
    )(n1t, *parts)


def toeplitz(base_ref):
    row = lax.broadcasted_iota(jnp.int32, (T, T), 0)
    col = lax.broadcasted_iota(jnp.int32, (T, T), 1)
    count = base_ref.shape[1]
    rolled = [
        pltpu.roll(jnp.broadcast_to(base_ref[0, u:u + 1, :], (T, T)), 0, 1, stride=1, stride_axis=0)
        for u in range(count)
    ]
    return [jnp.where(col >= row, rolled[u], rolled[u + 1] if u + 1 < count else NEG) for u in range(count)]


def key_mask(len_ref, start):
    slot = start + lax.broadcasted_iota(jnp.int32, (T, 1), 0)
    return jnp.where(slot < len_ref[0], 0.0, NEG).astype(F32)


def attend_kernel(me_ref, len_ref, base_ref, q_ref, k_ref, v_ref, o_ref, lt_ref, g_ref):
    heads, tiles = base_ref.shape[:2]
    keys = [k_ref[h].T for h in range(heads)]
    for h in range(heads):
        for u, t in enumerate(toeplitz(base_ref.at[h:h + 1])):
            g_ref[h, u * T:(u + 1) * T, :] = t

    def scores(h, b):
        nk = (b + 1) * T
        q = q_ref[h, :, b * T:nk] * BF(HEAD_DIM ** -0.5)
        s = dot(keys[h][:nk], q) + g_ref[h, (tiles - 1 - b) * T:, :]
        if b == tiles - 1:
            s = jnp.concatenate([s[:b * T], s[b * T:] + key_mask(len_ref, b * T)], axis=0)
        return s, jnp.max(s, axis=0, keepdims=True)

    order = [(h, b) for b in range(tiles) for h in range(heads)]
    ahead = scores(*order[0])
    for n, (h, b) in enumerate(order):
        s, m = ahead
        if n + 1 < len(order):
            ahead = scores(*order[n + 1])
        sl = slice(b * T, (b + 1) * T)
        p = jnp.exp(s - m)
        total = jnp.sum(p, axis=0, keepdims=True)
        o = dot(v_ref[h, :, :(b + 1) * T], p.astype(BF))
        o_ref[h, :, sl] = (o * (1.0 / total)).astype(BF)
        lt_ref[h, :, sl] = m + jnp.log(total)


def head_place(h, me_ref):
    return jnp.bitwise_xor(h // 2, me_ref[0]) * 2 + h % 2


def attend(me, lengths, base, qkv):
    rows = qkv.shape[-1]
    tiles = rows // T
    pairs = HEADS // 2
    block = (2, HEAD_DIM, rows)
    at = lambda off: pl.BlockSpec(block, lambda h, m: (h + off, 0, 0))
    return pl.pallas_call(
        attend_kernel, name="attend",
        grid_spec=pltpu.PrefetchScalarGridSpec(
            num_scalar_prefetch=1, grid=(pairs,),
            in_specs=[SMEM, pl.BlockSpec((2, tiles, T), lambda h, m: (jnp.bitwise_xor(h, m[0]), 0, 0)), at(0), at(pairs), at(2 * pairs)],
            out_specs=[pl.BlockSpec(block, lambda h, m: (jnp.bitwise_xor(h, m[0]), 0, 0)),
                       pl.BlockSpec((2, 1, rows), lambda h, m: (h, 0, 0))],
            scratch_shapes=[pltpu.VMEM((2, rows, T), F32)]),
        out_shape=[shape_of((HEADS, HEAD_DIM, rows), BF), shape_of((HEADS, 1, rows), F32)],
        compiler_params=params(), cost_estimate=cost(30e9, 10e6),
    )(me, lengths, base, qkv, qkv, qkv)


def skew_sums(dg_ref, dist_ref):
    row = lax.broadcasted_iota(jnp.int32, (T, T), 0)
    col = lax.broadcasted_iota(jnp.int32, (T, T), 1)
    for u in range(dist_ref.shape[1]):
        z = jnp.where(col >= row, dg_ref[u * T:(u + 1) * T, :], dg_ref[(u - 1) * T:u * T, :] if u else 0.0)
        acc = z[0:8]
        for g in range(1, T // 8):
            acc = acc + pltpu.roll(z[8 * g:8 * g + 8], T - 8 * g, 1)
        tot = acc[0:1]
        for r in range(1, 8):
            tot = tot + pltpu.roll(acc[r:r + 1], T - r, 1)
        dist_ref[0, u:u + 1, :] = tot


def attend_back_kernel(me_ref, len_ref, base_ref, q_ref, k_ref, v_ref, o_ref, do_ref, lt_ref,
                       dq_ref, dk_ref, dv_ref, dist_ref, g_ref, dg_ref, dk_s, dv_s):
    tiles = base_ref.shape[1]
    scale = HEAD_DIM ** -0.5
    for u, t in enumerate(toeplitz(base_ref)):
        g_ref[u * T:(u + 1) * T, :] = t
    kt = k_ref[0]
    k = kt.T
    v = v_ref[0].T

    def scores(b):
        nk = (b + 1) * T
        sl = slice(b * T, nk)
        q = q_ref[0, :, sl] * BF(scale)
        do = do_ref[0, :, sl]
        inner = jnp.sum(do.astype(F32) * o_ref[0, :, sl].astype(F32), axis=0, keepdims=True)
        s = dot(k[:nk], q) + g_ref[(tiles - 1 - b) * T:, :]
        if b == tiles - 1:
            s = jnp.concatenate([s[:b * T], s[b * T:] + key_mask(len_ref, b * T)], axis=0)
        p = jnp.exp(s - lt_ref[0, :, sl])
        ds = p * (dot(v[:nk], do) - inner)
        return q, do, p.astype(BF), ds

    ahead = scores(tiles - 1)
    for b in range(tiles - 1, -1, -1):
        q, do, pb, ds = ahead
        if b:
            ahead = scores(b - 1)
        nk = (b + 1) * T
        low = (tiles - 1 - b) * T
        dsb = ds.astype(BF)
        dq_ref[0, :, b * T:nk] = (dot(kt[:, :nk], dsb) * scale).astype(BF)
        dvp = dot(do, pb, NT)
        dkp = dot(q, dsb, NT)
        if b == tiles - 1:
            dk_s[...] = dkp
            dv_s[...] = dvp
            dg_ref[...] = ds
        else:
            dk_s[:, :nk] += dkp
            dv_s[:, :nk] += dvp
            dg_ref[low:, :] += ds
    dk_ref[0] = dk_s[...].astype(BF)
    dv_ref[0] = dv_s[...].astype(BF)
    skew_sums(dg_ref, dist_ref)


def attend_back(me, lengths, base, qkv, o, do, lt, first, count, deps=()):
    rows = qkv.shape[-1]
    tiles = rows // T
    block = (1, HEAD_DIM, rows)
    at = lambda off: pl.BlockSpec(block, lambda h, m: (h + off + first, 0, 0))
    placed = pl.BlockSpec(block, lambda h, m: (head_place(h + first, m), 0, 0))
    out = pl.BlockSpec(block, lambda h, m: (h, 0, 0))
    return pl.pallas_call(
        with_deps(attend_back_kernel, 9, len(deps)), name="attend_back",
        grid_spec=pltpu.PrefetchScalarGridSpec(
            num_scalar_prefetch=1, grid=(count,),
            in_specs=[SMEM, pl.BlockSpec((1, tiles, T), lambda h, m: (head_place(h + first, m), 0, 0)), at(0), at(HEADS), at(2 * HEADS),
                      placed, placed, pl.BlockSpec((1, 1, rows), lambda h, m: (h + first, 0, 0))] + [ANY] * len(deps),
            out_specs=[out, out, out, pl.BlockSpec((1, tiles, T), lambda h, m: (h, 0, 0))],
            scratch_shapes=[pltpu.VMEM((rows, T), F32), pltpu.VMEM((rows, T), F32),
                            pltpu.VMEM((HEAD_DIM, rows), F32), pltpu.VMEM((HEAD_DIM, rows), F32)]),
        out_shape=[shape_of((count, HEAD_DIM, rows), BF)] * 3 + [shape_of((count, tiles, T), F32)],
        compiler_params=params(), cost_estimate=cost(2.4e9 * count, 1.2e6 * count),
    )(me, lengths, base, qkv, qkv, qkv, o, do, lt, *deps)


def middle_kernel(me_ref, at_ref, x_ref, gain_ref, shift_ref, *refs):
    parts, (mid_ref, n2_ref, n2t_ref, abs_s) = refs[:8], refs[8:]
    me = me_ref[0]
    w = jnp.concatenate([r[...] for r in in_order(parts)], axis=0)
    mid = x_ref[...].astype(F32) + dot(at_ref[...], w, TN)
    mid_ref[...] = mid
    hat, _ = normalise(mid)
    abs_s[...] = hat * gain_ref[...] + shift_ref[...]
    for r in range(8):
        sl = slice(r * 128, (r + 1) * 128)
        part = abs_s[:, pl.ds(block_of(me, r), 128)].astype(BF)
        n2_ref[:, sl] = part
        n2t_ref[sl, :] = part.T


def middle_of(me, at, x, gain, shift, parts, deps=()):
    rows, width = x.shape
    tile = pl.BlockSpec((T, width), lambda i: (i, 0))
    turned = pl.BlockSpec((width, T), lambda i: (0, i))
    return pl.pallas_call(
        with_deps(middle_kernel, 5 + len(parts), len(deps)), grid=(rows // T,), name="middle",
        in_specs=[SMEM, turned, tile, resident((1, width)), resident((1, width))] + [last_block(p, width) for p in parts]
        + [ANY] * len(deps),
        out_specs=[tile, tile, turned],
        out_shape=[shape_of((rows, width), F32), shape_of((rows, width), BF), shape_of((width, rows), BF)],
        scratch_shapes=[pltpu.VMEM((T, width), F32)],
        compiler_params=params(), cost_estimate=cost(2 * rows * width * width, 14e6),
    )(me, at, x, gain, shift, *parts, *deps)


def gelu_parts(x):
    a = jnp.abs(x)
    t = 1.0 / (1.0 + a * (0.3275911 * 0.7071067811865476))
    e = jnp.exp(x * x * -0.5)
    poly = t * (0.127414796 + t * (-0.142248368 + t * (0.7107068705 + t * (-0.7265760135 + t * 0.5307027145))))
    q = poly * e
    phi = jnp.where(x >= 0.0, 1.0 - q, q)
    return x * phi, phi + x * (e * 0.3989422804014327)


def feed_kernel(chunks, stacked, counts, me_ref, n2_h, n2t_h, og_h, w_h, *refs):
    carried, deps, n_out = counts
    carry, refs = refs[:carried], refs[carried + deps:]
    outs, refs = refs[:n_out], refs[n_out:]
    n2_v, n2t_v, og_v, w_v, g_v, hid_v, send_v, keep_v, sem_in, sem_out = refs
    me = me_ref[0]
    shard = [jnp.bitwise_xor(me, r) for r in range(8)]
    loads = [(n2_h, n2_v)]
    for part in (slice(0, 128), slice(128, 256)):
        loads += [(w_h.at[shard[r], chunks[0], part, :], w_v.at[r, 0, part, :]) for r in range(8)]
        if part.start == 0:
            loads.append((og_h, og_v))
    early = (9, 18)
    for k, c in enumerate(chunks[1:]):
        loads += [(w_h.at[shard[r], c], w_v.at[r, k + 1]) for r in range(8)]
    loads += list(zip(carry, (g_v,))) + [(n2t_h, n2t_v)]
    copies = [pltpu.make_async_copy(a, b, sem_in.at[i]) for i, (a, b) in enumerate(loads)]
    for x in copies:
        x.start()
    for x in copies[:early[0]]:
        x.wait()
    stores = []

    def store(a, b):
        stores.append(pltpu.make_async_copy(a, b, sem_out.at[len(stores)]))
        stores[-1].start()

    n2 = n2_v[...]
    steps = 2 * len(chunks)

    for t in range(steps):
        k, u = t // 2, t % 2
        offs = [block_of(me, 4 * u + j) for j in range(4)]
        wi = jnp.concatenate([w_v[:, k, :128, pl.ds(o, 128)].reshape(1024, 128) for o in offs], axis=1)
        hid, slope = gelu_parts(dot(n2, wi))
        hid = hid.astype(BF)
        if t == 0:
            for x in copies[early[0]:early[1]]:
                x.wait()
            og = og_v[...]
        wd = w_v[4 * u:4 * u + 4, k, 128:, :].reshape(512, 1024)
        pre = (dot(og, wd, NT) * slope).astype(BF)
        hid_v[:, t * 512:(t + 1) * 512] = hid
        store(hid_v.at[:, t * 512:(t + 1) * 512], outs[1].at[:, t * 512:(t + 1) * 512])
        if t == 0:
            for x in copies[early[1]:]:
                x.wait()
        if not carried and t == 0:
            g_v[...] = dot(pre, wi, NT)
        else:
            g_v[...] += dot(pre, wi, NT)
        if t == steps - 1:
            store(g_v, outs[0])
        dwi = dot(n2t_v[...], pre).astype(BF)
        for r in range(8):
            for j, o in enumerate(offs):
                (send_v if r % 2 else keep_v)[k, r // 2, :128, pl.ds(o, 128)] = dwi[r * 128:(r + 1) * 128, j * 128:(j + 1) * 128]
        if u == 1 and not stacked:
            for half, out in ((send_v, outs[2]), (keep_v, outs[3])):
                for b in range(4):
                    store(half.at[k, :, :128, b * 256:(b + 1) * 256], out.at[:, 8 * k + b])
        dwd = dot(hid, og, TN).astype(BF)
        for j in range(4):
            r = 4 * u + j
            (send_v if r % 2 else keep_v)[k, r // 2, 128:, :] = dwd[j * 128:(j + 1) * 128]
        if u == 1:
            if stacked:
                for r in range(8):
                    store((send_v if r % 2 else keep_v).at[k, r // 2], outs[2].at[shard[r], k])
            else:
                for half, out in ((send_v, outs[2]), (keep_v, outs[3])):
                    for b in range(4):
                        store(half.at[k, :, 128:, b * 256:(b + 1) * 256], out.at[:, 8 * k + 4 + b])
    for x in stores:
        x.wait()


def feed(chunks, stacked, me, n2, n2t, og, w, carry=(), deps=()):
    rows, width = n2.shape
    n = len(chunks)
    half = (n, 4, 256, 1024)
    grads = [(8, n, 256, 1024)] if stacked else [(4, 8 * n, 128, 256)] * 2
    counts = (len(carry), len(deps), 2 + len(grads))
    return pl.pallas_call(
        functools.partial(feed_kernel, chunks, stacked, counts), name="feed",
        in_specs=[SMEM] + [ANY] * (4 + len(carry) + len(deps)), out_specs=[ANY] * counts[2],
        out_shape=[shape_of((rows, width), F32), shape_of((rows, 1024 * n), BF)] + [shape_of(g, BF) for g in grads],
        scratch_shapes=[pltpu.VMEM((rows, width), BF), pltpu.VMEM((width, rows), BF), pltpu.VMEM((rows, width), BF),
                        pltpu.VMEM((8, n, 256, 1024), BF), pltpu.VMEM((rows, width), F32), pltpu.VMEM((rows, 1024 * n), BF),
                        pltpu.VMEM(half, BF), pltpu.VMEM(half, BF),
                        pltpu.SemaphoreType.DMA((20 + 8 * n,)), pltpu.SemaphoreType.DMA((20 * n + 1,))],
        compiler_params=params(), cost_estimate=cost(18e9 * n, 25e6),
    )(me, n2, n2t, og, w, *carry, *deps)


def output_kernel(me_ref, len_ref, mid_ref, *refs):
    hids, (w0_h, w1_h), (out_ref, w_v, sem) = refs[:-5], refs[-5:-3], refs[-3:]
    me = me_ref[0]
    i = pl.program_id(0)
    rows = mid_ref.shape[0]

    @pl.when(i == 0)
    def _():
        copies = []
        for k, h in enumerate((w0_h, w1_h)):
            for c in range(2):
                for r in range(8):
                    n = len(copies)
                    copies.append(pltpu.make_async_copy(
                        h.at[jnp.bitwise_xor(me, r), c, 128:, :], w_v.at[(2 * k + c) * 8 + r], sem.at[n]))
        for x in copies:
            x.start()
        for x in copies:
            x.wait()

    hid = jnp.concatenate([h[...] for h in hids], axis=1)
    total = mid_ref[...] + dot(hid, w_v[...].reshape(-1, w_v.shape[2]))
    slot = i * rows + lax.broadcasted_iota(jnp.int32, (rows, 1), 0)
    out_ref[...] = jnp.where(slot < len_ref[0], total, 0.0).astype(BF)


def output(me, lengths, mid, hids, w, deps=()):
    rows, width = mid.shape
    tile = pl.BlockSpec((T, width), lambda i: (i, 0))
    return pl.pallas_call(
        with_deps(output_kernel, 5 + len(hids), len(deps)), grid=(rows // T,), name="output",
        in_specs=[SMEM, SMEM, tile] + [pl.BlockSpec((T, h.shape[1]), lambda i: (i, 0)) for h in hids] + [ANY] * (2 + len(deps)),
        out_specs=tile, out_shape=shape_of((rows, width), BF),
        scratch_shapes=[pltpu.VMEM((32, 128, width), BF), pltpu.SemaphoreType.DMA((32,))],
        compiler_params=params(), cost_estimate=cost(9e9, 20e6),
    )(me, lengths, mid, *hids, *w, *deps)


def norm_back(hat, rstd, grad, gain):
    t = grad * gain
    return (t - jnp.mean(t, axis=-1, keepdims=True) - hat * jnp.mean(t * hat, axis=-1, keepdims=True)) * rstd


def middle_back_kernel(me_ref, mid_ref, g_ref, og_ref, at_ref, gain_ref, *refs):
    parts, (mg_ref, do_ref, send_ref, keep_ref, vec_ref, abs_s, acc_s) = refs[:8], refs[8:]
    me = me_ref[0]
    i = pl.program_id(0)
    for r in range(8):
        abs_s[:, pl.ds(block_of(me, r), 128)] = g_ref[:, r * 128:(r + 1) * 128]
    grad = abs_s[...]
    hat, rstd = normalise(mid_ref[...])
    sums = jnp.concatenate([jnp.sum(grad * hat, axis=0, keepdims=True), jnp.sum(grad, axis=0, keepdims=True)], axis=0)
    mg = og_ref[...].astype(F32) + norm_back(hat, rstd, grad, gain_ref[...])
    mg_ref[...] = mg
    branch = mg.astype(BF)
    w = jnp.concatenate([r[...] for r in in_order(parts)], axis=0)
    do_ref[...] = dot(w, branch, NT).astype(BF)
    dw = dot(at_ref[...], branch)

    @pl.when(i == 0)
    def _():
        vec_ref[...] = sums
        acc_s[...] = dw

    @pl.when(i > 0)
    def _():
        vec_ref[...] += sums
        acc_s[...] += dw

    @pl.when(i == pl.num_programs(0) - 1)
    def _():
        for r in range(8):
            for b in range(4):
                (send_ref if r % 2 else keep_ref)[r // 2, b] = acc_s[r * 128:(r + 1) * 128, b * 256:(b + 1) * 256].astype(BF)


def middle_back(me, mid, g, og, at, gain, parts, deps=()):
    rows, width = mid.shape
    tile = pl.BlockSpec((T, width), lambda i: (i, 0))
    turned = pl.BlockSpec((width, T), lambda i: (0, i))
    block = (4, 4, 128, 256)
    return pl.pallas_call(
        with_deps(middle_back_kernel, 6 + len(parts), len(deps)), grid=(rows // T,), name="middle_back",
        in_specs=[SMEM, tile, tile, tile, turned, resident((1, width))] + [last_block(p, width) for p in parts] + [ANY] * len(deps),
        out_specs=[tile, turned, resident(block), resident(block), resident((2, width))],
        out_shape=[shape_of((rows, width), F32), shape_of((width, rows), BF), shape_of(block, BF), shape_of(block, BF),
                   shape_of((2, width), F32)],
        scratch_shapes=[pltpu.VMEM((T, width), F32), pltpu.VMEM((width, width), F32)],
        compiler_params=params(), cost_estimate=cost(4 * rows * width * width, 24e6),
    )(me, mid, g, og, at, gain, *parts, *deps)


class Part:
    def __init__(self, array, start=0, count=None):
        self.array, self.start = array, start
        self.shape = ((array.shape[0] - start) if count is None else count,) + tuple(array.shape[1:])
        self.dtype = array.dtype

    def part(self, start, count):
        return Part(self.array, self.start + start, count)


def staged_kernel(steps, places, n_in, n_dep, n_out, where_ref, *refs):
    sources, refs = refs[:n_in], refs[n_in + n_dep:]
    dests, refs = refs[:n_out], refs[n_out:]
    n_kept = len(places)
    held, kept, sem_in, sem_out = refs[:n_in], refs[n_in:n_in + n_kept], refs[-2], refs[-1]
    loads = []
    for ins, _, _ in steps:
        for p in ins:
            k = len(loads)
            loads.append(pltpu.make_async_copy(sources[k].at[p.start:p.start + p.shape[0]], held[k], sem_in.at[k]))
    for c in loads:
        c.start()
    stores = []
    a = b = 0
    for ins, outs, fn in steps:
        for c in loads[a:a + len(ins)]:
            c.wait()
        fn(where_ref, held[a:a + len(ins)], kept[b:b + len(outs)])
        for k in range(b, b + len(outs)):
            n, start = places[k]
            stores.append(pltpu.make_async_copy(kept[k], dests[n].at[start:start + kept[k].shape[0]], sem_out.at[k]))
            stores[-1].start()
        a += len(ins)
        b += len(outs)
    for c in stores:
        c.wait()


def staged(where, steps, deps=()):
    steps = [([v if isinstance(v, Part) else Part(v) for v in ins], outs, fn) for ins, outs, fn in steps]
    parts = [v for ins, _, _ in steps for v in ins]
    flat = [o for _, outs, _ in steps for o in outs]
    arrays, places, by_way = [], [], {}
    for way, shape, kind in flat:
        if way is None:
            places.append((len(arrays), 0))
            arrays.append(shape_of(shape, kind))
            continue
        key = (way,) + tuple(shape[1:]) + (kind,)
        if key not in by_way:
            by_way[key] = len(arrays)
            arrays.append(shape_of((0,) + tuple(shape[1:]), kind))
        n = by_way[key]
        places.append((n, arrays[n].shape[0]))
        arrays[n] = shape_of((arrays[n].shape[0] + shape[0],) + tuple(shape[1:]), kind)
    out = pl.pallas_call(
        functools.partial(staged_kernel, steps, places, len(parts), len(deps), len(arrays)), name="staged",
        in_specs=[SMEM] + [ANY] * (len(parts) + len(deps)), out_specs=[ANY] * len(arrays), out_shape=arrays,
        scratch_shapes=[pltpu.VMEM(v.shape, v.dtype) for v in parts] + [pltpu.VMEM(o[1], o[2]) for o in flat]
        + [pltpu.SemaphoreType.DMA((len(parts),)), pltpu.SemaphoreType.DMA((len(flat),))],
        compiler_params=params(), cost_estimate=cost(3e9, 10e6),
    )(where, *(p.array for p in parts), *deps)
    sent = list(out)
    for key, n in by_way.items():
        sent[n] = send(out[n], key[0])
    flat = [[Part(v, start, o[1][0]) for v in sent[n]] if o[0] == "turns" else Part(sent[n], start, o[1][0])
            for (n, start), o in zip(places, flat)]
    result = []
    for _, o, _ in steps:
        result.append(flat[:len(o)])
        flat = flat[len(o):]
    return result, tuple(out)


def send(v, way):
    if way in ("core", "x", "y", "both"):
        return flip(v, {"core": 1, "x": 2, "y": 4, "both": 6}[way])
    if way == "turns":
        return copy_turns(v, 4)
    k = {"pair": 1, "far": 2}[way]
    return lax.ppermute(v, "rep", [(i, i ^ k) for i in range(4)])


def plus(*refs):
    total = refs[0].astype(F32)
    for r in refs[1:]:
        total = total + r.astype(F32)
    return total


def project_back(n1t, three, way):
    block = (12, 128, 256)

    def fn(_, ins, outs):
        n1 = ins[0][...]
        for j in range(3):
            dw = dot(n1, ins[1 + j][...], NT).astype(BF)
            for r in range(8):
                outs[r % 2 == 0][r // 2 * 3 + j] = dw[r * 128:(r + 1) * 128]

    return [n1t, *three], [(way, block, BF), (None, block, BF)], fn


def put(out, v):
    nb, rows = v.shape[0], out.shape[1]
    for k in range(out.shape[0] // nb):
        out[k * nb:(k + 1) * nb] = v[:, k * rows:(k + 1) * rows]


def whole(v):
    nb = v.shape[0] * v.shape[1] // 128
    return jnp.concatenate([v[k * nb:(k + 1) * nb] for k in range(128 // v.shape[1])], axis=1)


class Piece:
    def __init__(self, nb, keep, got, straight, copies):
        self.nb, self.keep, self.got = nb, keep, got
        self.plan = ["straight", "straight_sum"] if straight else ["sums", "second", "shard"]
        self.plan += {"halves": ["quarter", "quarter_back", "half_back"], "pairs": ["far"], "turns": []}[copies]
        self.copies = copies

    def step(self):
        return getattr(self, self.plan.pop(0))()

    def take(self, result):
        self.got = result

    def sums(self):
        nb = self.nb

        def fn(_, ins, outs):
            k, g = ins
            for out, half, pair in zip(outs, (0, 1, 0, 1), ((1, 3), (2, 3), (0, 2), (0, 1))):
                rows = slice(half * 64, half * 64 + 64)
                for n, j in enumerate(pair):
                    at = slice(j * nb, (j + 1) * nb)
                    out[n * nb:(n + 1) * nb] = plus(k[at, rows, :], g[at, rows, :]).astype(BF)

        out = (2 * nb, 64, 256)
        return [self.keep, self.got], [("x", out, BF), ("y", out, BF), (None, out, BF), (None, out, BF)], fn

    def second(self):
        nb = self.nb
        gx, gy, a, b = self.got
        self.rest = (a.part(0, nb), gx.part(0, nb), b.part(0, nb), gy.part(0, nb))

        def fn(_, ins, outs):
            outs[0][...] = plus(ins[0][...], ins[1][...]).astype(BF)
            outs[1][...] = plus(ins[2][...], ins[3][...]).astype(BF)

        out = (nb, 64, 256)
        ins = [v.part(nb, nb) for v in (a, gx, b, gy)]
        return ins, [("y", out, BF), ("x", out, BF)], fn

    def shard(self):
        a, gx, b, gy = self.rest

        def fn(where, ins, outs):
            a = plus(ins[0][...], ins[1][...], ins[2][...]).astype(BF)
            b = plus(ins[3][...], ins[4][...], ins[5][...]).astype(BF)
            self.first_copies(where, outs, a, b)

        return [a, gx, self.got[0], b, gy, self.got[1]], self.first_outs(), fn

    def straight(self):
        nb = self.nb

        def fn(_, ins, outs):
            for out, j in zip(outs, (1, 2, 3, 0)):
                at = slice(j * nb, (j + 1) * nb)
                put(out, plus(ins[0][at], ins[1][at]).astype(BF))

        out = (2 * nb, 64, 256)
        return [self.keep, self.got], [(way, out, BF) for way in ("x", "y", "both", None)], fn

    def straight_sum(self):
        nb = self.nb

        def fn(where, ins, outs):
            v = plus(*(r[...] for r in ins)).astype(BF)
            self.first_copies(where, outs, v[:nb], v[nb:])

        return list(self.got), self.first_outs(), fn

    def first_outs(self):
        nb = self.nb
        out = ((nb if self.copies == "halves" else 2 * nb), 64, 256)
        return [("turns" if self.copies == "turns" else "pair", out, BF), (None, out, BF)]

    def first_copies(self, where, outs, a, b):
        nb = self.nb
        if self.copies == "halves":
            odd = where[1] == 1
            outs[0][...] = jnp.where(odd, a, b)
            outs[1][...] = jnp.where(odd, b, a)
        else:
            for out in outs:
                out[:nb] = a
                out[nb:] = b

    def far(self):
        def fn(_, ins, outs):
            v = whole(plus(ins[0][...], ins[1][...]).astype(BF))
            for out in outs:
                put(out, v)

        out = (4 * self.nb, 32, 256)
        return list(self.got), [("far", out, BF), (None, out, BF)], fn

    def quarter(self):
        def fn(where, ins, outs):
            a = plus(ins[0][:, :32], ins[1][:, :32]).astype(BF)
            b = plus(ins[0][:, 32:], ins[1][:, 32:]).astype(BF)
            high = where[2] == 1
            outs[0][...] = jnp.where(high, a, b)
            outs[1][...] = jnp.where(high, b, a)

        out = (self.nb, 32, 256)
        return list(self.got), [("far", out, BF), (None, out, BF)], fn

    def quarter_back(self):
        def fn(_, ins, outs):
            v = plus(ins[0][...], ins[1][...]).astype(BF)
            outs[0][...] = v
            outs[1][...] = v

        out = (self.nb, 32, 256)
        return list(self.got), [("far", out, BF), (None, out, BF)], fn

    def half_back(self):
        def fn(where, ins, outs):
            high = where[2] == 1
            got, mine = ins[0][...], ins[1][...]
            for out in outs:
                out[:, :32] = jnp.where(high, got, mine)
                out[:, 32:] = jnp.where(high, mine, got)

        out = (self.nb, 64, 256)
        return list(self.got), [("pair", out, BF), (None, out, BF)], fn

    def final(self):
        nb, copies = self.nb, self.copies
        ins = (list(self.got[0]) + [self.got[1]]) if copies == "turns" else list(self.got)

        def value(where, ins, b):
            if copies != "halves":
                rows = ins[0].shape[1]
                return jnp.concatenate([plus(*(r[k * nb + b] for r in ins)) for k in range(128 // rows)]).astype(BF).astype(F32)
            odd = where[1] == 1
            got, mine = ins[0][b].astype(F32), ins[1][b].astype(F32)
            return jnp.concatenate([jnp.where(odd, got, mine), jnp.where(odd, mine, got)])

        return ins, value


def finish_kernel(groups, me_ref, x_ref, mg_ref, gain_ref, *refs):
    parts, refs = refs[:8], refs[8:]
    grads, (ig_ref, vec_ref, abs_s) = refs[:3 * groups], refs[3 * groups:]
    me = me_ref[0]
    i = pl.program_id(0)
    rows, width = x_ref.shape
    w = jnp.concatenate([r[...] for r in in_order(parts)], axis=0)
    pg = jnp.concatenate([grads[3 * g + j][...] for j in range(3) for g in range(groups)], axis=0)
    total = dot(pg, w, TT)
    for r in range(8):
        abs_s[:, pl.ds(block_of(me, r), 128)] = total[:, r * 128:(r + 1) * 128]
    grad = abs_s[...]
    hat, rstd = normalise(x_ref[...].astype(F32))
    sums = jnp.concatenate([jnp.sum(grad * hat, axis=0, keepdims=True), jnp.sum(grad, axis=0, keepdims=True)], axis=0)
    ig_ref[...] = mg_ref[...] + norm_back(hat, rstd, grad, gain_ref[...])

    @pl.when(i == 0)
    def _():
        vec_ref[...] = sums

    @pl.when(i > 0)
    def _():
        vec_ref[...] += sums


def finish(me, x, mg, gain, parts, grads, deps=()):
    rows, width = x.shape
    tile = pl.BlockSpec((T, width), lambda i: (i, 0))
    return pl.pallas_call(
        with_deps(functools.partial(finish_kernel, len(grads) // 3), 4 + len(parts) + len(grads), len(deps)),
        grid=(rows // T,), name="finish",
        in_specs=[SMEM, tile, tile, resident((1, width))] + [resident((p.shape[0], 3 * width)) for p in parts]
        + [pl.BlockSpec((g.shape[0], T), lambda i: (0, i)) for g in grads] + [ANY] * len(deps),
        out_specs=[tile, resident((2, width))],
        out_shape=[shape_of((rows, width), F32), shape_of((2, width), F32)],
        scratch_shapes=[pltpu.VMEM((T, width), F32)],
        compiler_params=params(), cost_estimate=cost(6 * rows * width * width, 34e6),
    )(me, x, mg, gain, *parts, *grads, *deps)


def flip(v, k):
    return lax.ppermute(v, "fsdp", [(i, i ^ k) for i in range(GROUPS)])


def xor_rows(v, me):
    for k in (1, 2, 4):
        turned = v.reshape((8 // (2 * k), 2, k) + v.shape[1:])[:, ::-1].reshape(v.shape)
        v = jnp.where((me & k) != 0, turned, v)
    return v


def split_full(full):
    m = full.shape[0] // 8
    return [full[r * m:(r + 1) * m] for r in PLACES]


def vector_sums(vec_one, vec_two, dists, buckets):
    def fn(where, ins, outs):
        by = jnp.concatenate([jnp.concatenate([d[:, u, :] for u in range(d.shape[1] - 1, -1, -1)], axis=1) for d in ins[2:-1]])
        onehot = (ins[-1][...] == lax.broadcasted_iota(jnp.int32, (BUCKETS, by.shape[1]), 0)).astype(F32)
        table = lax.dot_general(by, onehot, NT, precision=lax.Precision.HIGHEST, preferred_element_type=F32)
        table_s, row_s = outs[2:]
        table_s[...] = jnp.concatenate([jnp.concatenate([table[2 * r:2 * r + 1], table[2 * r + 1:2 * r + 2]], axis=1) for r in range(8)])
        row_s[...] = jnp.zeros_like(row_s)
        for out in outs[:2]:
            out[...] = jnp.zeros_like(out)
        for r in range(8):
            at = pl.ds(block_of(where[0], r), 128)
            for k in range(4):
                row_s[k // 2:k // 2 + 1, k % 2 * 128:(k % 2 + 1) * 128] = ins[k // 2][k % 2:k % 2 + 1, at]
            row_s[2:3, :64] = table_s[pl.ds(jnp.bitwise_xor(where[0], r), 1), :]
            outs[1 - r % 2][r // 2, :16, :] = row_s[...].astype(BF)

    out = (4, 128, 256)
    return [vec_one, vec_two, *dists, buckets], [
        ("core", out, BF), (None, out, BF), (None, (8, 64), F32), (None, (16, 256), F32)], fn


def vector_result(piece):
    mine, value = piece.final()

    def fn(where, ins, outs):
        v = value(where, ins, 0)
        for k in range(4):
            outs[k][...] = v[k // 2:k // 2 + 1, k % 2 * 128:(k % 2 + 1) * 128]
        outs[4][...] = v[2:3, :64]

    return mine, [(None, (1, 128), F32)] * 4 + [(None, (1, 64), F32)], fn


def feed_result(one, pieces):
    finals = [p.final() for p in pieces]

    def fn(where, ins, outs):
        for c in range(2):
            base = c * 256
            for b in range(8):
                col = (b * CHUNKS + c) * 128
                outs[0][:, col:col + 128] = ins[0][base:base + 128, b * 128:(b + 1) * 128].astype(F32)
            outs[1][c * 128:(c + 1) * 128, :] = ins[0][base + 128:base + 256, :].astype(F32)
        at = 1
        for c, (mine, value) in zip((2, 3), finals):
            refs = ins[at:at + len(mine)]
            at += len(mine)
            for b in range(4):
                v = value(where, refs, b)
                for k in range(2):
                    col = ((2 * b + k) * CHUNKS + c) * 128
                    outs[0][:, col:col + 128] = v[:, k * 128:(k + 1) * 128]
                outs[1][c * 128:(c + 1) * 128, b * 256:(b + 1) * 256] = value(where, refs, 4 + b)

    return [one] + [v for mine, _ in finals for v in mine], [(None, (128, 4096), F32), (None, (512, 1024), F32)], fn


def project_result(out_piece, pieces):
    finals = [p.final() for p in [out_piece] + pieces]

    def fn(where, ins, outs):
        at = 0
        for g, (mine, value) in enumerate(finals):
            refs = ins[at:at + len(mine)]
            at += len(mine)
            for b in range(3 if g else 4):
                col = (b * HEAD_GROUPS + g - 1) * 256 if g else b * 256
                outs[0 if g else 1][:, col:col + 256] = value(where, refs, b)

    return [v for mine, _ in finals for v in mine], [(None, (128, 3072), F32), (None, (128, 1024), F32)], fn


def copy_turns(v, count):
    return [lax.ppermute(v, "rep", [(i, (i + k) % count) for i in range(count)]) for k in range(1, count)]


def per_device(n_fsdp, n_rep, inputs, lengths, bucket_table, ln1_gain, ln1_shift, w_qkv, rel_bias, w_out, ln2_gain, ln2_shift,
               w_in, w_down, cotangent):
    near = n_fsdp == GROUPS and n_rep == 4
    _, slots, width = inputs.shape
    hidden = w_in.shape[1]
    me = lax.axis_index("fsdp").astype(jnp.int32) if near else jnp.int32(0)
    me1 = me.reshape(1)
    x = inputs.reshape(slots, width)
    cot = cotangent.reshape(slots, width)
    full = lambda w: lax.all_gather(w, "fsdp", axis=0, tiled=True)

    if near:
        piece, own = lead(w_qkv, w_out, ln1_gain, ln1_shift, ln2_gain, ln2_shift, rel_bias)
        small = jnp.concatenate([own] + [flip(own, k) for k in (2, 4, 6)])
        small = jnp.stack([small, flip(small, 1)], axis=1).reshape(8, -1)
        r2, r4 = flip(piece, 2), flip(piece, 4)
        h2, h4 = halves(r2, r4)
        r6a, r6b = flip(h2, 4), flip(h4, 2)
        n1t, og, vecs, base = prepare(me1, lengths, x, cot, bucket_table[None], small, (h2, h4))
        ffn_w = [full(v.reshape(512, 1024)).reshape(8, 2, 256, 1024) for v in pack(w_in, w_down, (h2, h4))]
        parts = [piece, r2, r4, join(r6a, r6b, (n1t,))]
        parts = parts + [flip(v, 1) for v in parts]
    else:
        n = ln1_gain.shape[0]
        small = full(jnp.concatenate([ln1_gain, ln1_shift, ln2_gain, ln2_shift, rel_bias])[None])
        small = jnp.concatenate([small[:, i * n:(i + 1) * n].reshape(8, 128) for i in range(4)] + [small[:, 4 * n:].reshape(8, 64)], axis=1)
        n1t, og, vecs, base = prepare(me1, lengths, x, cot, bucket_table[None], small)
        parts = split_full(jnp.concatenate([full(w_qkv), full(w_out)], axis=1))
        wi_c = full(w_in).reshape(8, width // 8, 8, CHUNKS, 128)
        wd_c = full(w_down).reshape(8, CHUNKS, 128, width)
        chunk = [jnp.concatenate([wi_c[:, :, :, c].reshape(8, width // 8, 1024), wd_c[:, c]], axis=1) for c in range(CHUNKS)]
        ffn_w = [jnp.stack(chunk[2 * h:2 * h + 2], axis=1) for h in range(2)]
    n = ln1_gain.shape[0]
    gain_one, shift_one, gain_two, shift_two = (vecs[i:i + 1] for i in range(4))
    qkv = project(n1t, parts)
    o, lt = attend(me1, lengths, base, qkv)
    at = o.reshape(width, slots)
    mid, n2, n2t = middle_of(me1, at, x, gain_two, shift_two, parts)
    grads, dists = [], []
    rep = lax.axis_index("rep").astype(jnp.int32)
    where = jnp.stack([me, rep % 2, rep // 2])
    per = HEADS // HEAD_GROUPS
    last = ffn_w[1]

    def back(k, deps=()):
        *three, dist = attend_back(me1, lengths, base, qkv, o, do, lt, k * per, per, deps)
        three = [v.reshape(per * HEAD_DIM, slots) for v in three]
        grads.extend(three)
        dists.append(dist)
        return three

    def slot(pieces, before=(), after=(), deps=()):
        result, made = staged(where, list(before) + [p.step() for p in pieces] + list(after), deps)
        for p, r in zip(pieces, result[len(before):]):
            p.take(r)
        return result[:len(before)] + result[len(before) + len(pieces):], made

    g, hid1, one = feed((0, 1), True, me1, n2, n2t, og, ffn_w[0])
    if near:
        one = lax.psum_scatter(one.reshape(8 * 512, 1024), "fsdp", scatter_dimension=0, tiled=True)
        blocks = lambda v: v.reshape((-1,) + v.shape[2:])
        start = lambda nb, away, keep, *plan: Piece(nb, Part(blocks(keep)), Part(flip(blocks(away), 1)), *plan)
        g, hid2, away, keep = feed((0,), False, me1, n2, n2t, og, last, (g,))
        f2 = start(8, away, keep, False, "halves")
        g, hid3, away, keep = feed((1,), False, me1, n2, n2t, og, last, (g,))
        f3 = start(8, away, keep, False, "halves")
        _, made = slot([f2], deps=(g,))
        mg, do, away, keep, vec_two = middle_back(me1, mid, g, og, at, gain_two, parts, made)
        do = do.reshape(HEADS, HEAD_DIM, slots)
        wo = start(4, away, keep, False, "pairs")
        _, made = slot([f3], deps=(mg,))
        three = back(0, made)
        ((got, keep),), made = slot([f2, f3], [project_back(n1t, three, "core")], deps=(one,))
        one = lax.psum(one, "rep")
        q0 = Piece(3, keep, got, False, "pairs")
        three = back(1, made)
        ((got, keep),), made = slot([f2, f3, wo, q0], [project_back(n1t, three, "core")])
        q1 = Piece(3, keep, got, False, "pairs")
        three = back(2, made)
        ((got, keep),), made = slot([f2, f3, wo, q0, q1], [project_back(n1t, three, "core")])
        q2 = Piece(3, keep, got, False, "pairs")
        three = back(3, made)
        ((got, keep),), made = slot([f2, f3, wo, q0, q1, q2], [project_back(n1t, three, "core")])
        q3 = Piece(3, keep, got, True, "pairs")
        input_grad, vec_one = finish(me1, x, mg, gain_one, parts, grads, made)
        ((got, keep, *_),), made = slot([], [vector_sums(vec_one, vec_two, dists, bucket_table[None])])
        vec = Piece(1, keep, got, True, "pairs")
        came = lambda *pieces: tuple(p.got[0].array for p in pieces)
        _, made = slot([q3, q2, f2, f3, wo, q0, q1, vec], deps=(one,))
        outputs = output(me1, lengths, mid, [hid1, hid2, hid3], ffn_w, made)
        ((in_grad, down_grad),), made = slot([q3, vec, q2, q1], [], [feed_result(one, [f2, f3])], deps=(outputs,) + came(wo, q0))
        _, made = slot([q3, q2, vec], deps=came(q1))
        ((qkv_grad, out_g), tiny), _ = slot([], [project_result(wo, [q0, q1, q2, q3]), vector_result(vec)])
        in_grad, down_grad, qkv_grad, out_g = (v.array for v in (in_grad, down_grad, qkv_grad, out_g))
        tiny = [v.array[0] for v in tiny]
    else:
        g, hid2, two = feed((0, 1), True, me1, n2, n2t, og, last, (g,))
        mg, do, away, keep, vec_two = middle_back(me1, mid, g, og, at, gain_two, parts)
        do = do.reshape(HEADS, HEAD_DIM, slots)
        pieces = [staged(where, [project_back(n1t, back(k), None)])[0][0] for k in range(HEAD_GROUPS)]
        input_grad, vec_one = finish(me1, x, mg, gain_one, parts, grads)
        outputs = output(me1, lengths, mid, [hid1, hid2], ffn_w)
        onehot = (bucket_table[:, None] == lax.iota(jnp.int32, BUCKETS)[None, :]).astype(F32)
        distance_total = jnp.concatenate(dists)[:, ::-1].reshape(HEADS, slots)
        table_grad = jnp.dot(distance_total, onehot, precision=lax.Precision.HIGHEST, preferred_element_type=F32)
        vec = jnp.concatenate([v.reshape(n_fsdp, -1) for v in (vec_one[0], vec_one[1], vec_two[0], vec_two[1], table_grad)], axis=1)
        reduced = lambda v: lax.psum(lax.psum_scatter(v, "fsdp", scatter_dimension=0, tiled=True), "rep")
        tiny = reduced(vec)[0]
        tiny = [tiny[k * n:(k + 1) * n] for k in range(4)] + [tiny[4 * n:]]
        stack = jnp.concatenate([one, two], axis=1)
        in_grad = reduced(stack[:, :, :128].reshape(8, CHUNKS, 128, 8, 128).transpose(0, 2, 3, 1, 4).reshape(width, hidden))
        down_grad = reduced(stack[:, :, 128:].reshape(hidden, width))
        whole = lambda away, keep: jnp.stack([keep, away], axis=1).reshape((8,) + keep.shape[1:]).swapaxes(1, 2)
        out_g = reduced(whole(away, keep).reshape(width, width))
        columns = [whole(*(v.array.reshape(4, 3, 128, 256) for v in p)) for p in pieces]
        qkv_grad = reduced(jnp.stack(columns, axis=3).reshape(width, 3 * width))
    return (outputs.reshape(inputs.shape), input_grad.reshape(inputs.shape), tiny[0], tiny[1], qkv_grad.astype(F32),
            tiny[4], out_g.astype(F32), tiny[2], tiny[3], in_grad.astype(F32), down_grad.astype(F32))


def solution(mesh):
    rows = P(("rep", "fsdp"), None, None)
    vec = P("fsdp")
    mat = P("fsdp", None)
    return jax.shard_map(
        functools.partial(per_device, mesh.shape["fsdp"], mesh.shape["rep"]),
        mesh=mesh,
        in_specs=(rows, P(("rep", "fsdp")), P(), vec, vec, mat, vec, mat, vec, vec, mat, mat, rows),
        out_specs=(rows, rows, vec, vec, mat, vec, mat, vec, vec, mat, mat),
        check_vma=False,
    )
```
